32 devices in a mesh: groups: 2 (over y), dp: 4 (over z), tensor: 4 (over x, core).
Axes of the slice: x: 2, y: 2, z: 4, core: 2. Of those that a mesh axis runs over, the one named last changes fastest.
Arguments:
- tokens: bfloat16 [1024, 1792], P(('groups', 'dp')), parts along dimension 0, may hold values from -6 to 6
- expert_ids: int32 [1024, 8], P(('groups', 'dp')), parts along dimension 0, may hold values from 0 to 31, all different within a row; in each aligned block of 128 rows (0 to 127, 128 to 255, ...) at most 48 rows name the same one
- route_gates: float32 [1024, 8], P(('groups', 'dp')), parts along dimension 0, may hold values from 0.05 to 0.5
- shared_gate_vec: bfloat16 [1792], replicated, may hold values from -0.125 to 0.125
- w_shared_gate: bfloat16 [1792, 10240], P('dp', 'tensor'), may hold values from -0.125 to 0.125
- w_shared_up: bfloat16 [1792, 10240], P('dp', 'tensor'), may hold values from -0.125 to 0.125
- w_shared_down_t: bfloat16 [1792, 10240], P('dp', 'tensor'), may hold values from -0.0625 to 0.0625
- w_expert_gate_t: bfloat16 [32, 2560, 1792], P('dp', 'tensor'), may hold values from -0.125 to 0.125
- w_expert_up_t: bfloat16 [32, 2560, 1792], P('dp', 'tensor'), may hold values from -0.125 to 0.125
- w_expert_down: bfloat16 [32, 2560, 1792], P('dp', 'tensor'), may hold values from -0.125 to 0.125
Outputs:
- moe_out: bfloat16 [1024, 1792], P(('groups', 'dp'), 'tensor'), parts along dimension 0
The draws below stay inside these ranges and needn't reach their ends.
There are 2 independent parts, one for each index of `groups`. The reference program is written for one: setup_inputs(seed, part) draws one part's arguments, and reference() takes and returns one part's arrays. A program takes and returns all parts, laid end to end along the dimension named above; an argument that names none is the same for every part. Nothing has to cross between parts.
Inputs may be any that keep to these rules, and one draw needn't show every extreme that they name: `expert_ids`: each row names 8 different experts. Within the rows of one index of dp (aligned blocks of 128 rows), no expert is named more than 48 times, a bound that some block reaches.
All inputs are finite; a program needn't handle non-finite values.
Results may differ from the reference program's by a relative error of at most 0.0049.
Values may be sent and summed in bfloat16 or wider, within the bound.
No kernel may reach another device: no remote copies, remote signals or barrier semaphores. Data moves between devices by JAX's collectives and lax.ppermute only.
A program may use at most 256 MiB of HBM per device.

```python
import math
import jax
import jax.numpy as jnp
import numpy as np
from jax import lax

D = 1792
FF_S = 10240
FF_E = 2560
EXPERTS = 32
TOP = 8
TOK_DP = 128
CAP = 48
TOKENS = 512
N_DP = 4


def steps_of(own_key, shape, pieces, least, largest):
    factor_of = 1.0
    for position, shards_of in pieces:
        heights = jax.random.uniform(jax.random.fold_in(jax.random.fold_in(own_key, 6), position), (shards_of,), jnp.float32, least / len(pieces), largest / len(pieces))
        factor_of = factor_of * jnp.repeat(jnp.exp(heights), shape[position] // shards_of).reshape((-1,) + (1,) * (len(shape) - 1 - position))
    return factor_of


def assign_block(own_key, own, number, rows, count, top, most, lean):
    ranking = jax.random.permutation(own_key, count)
    crowded, ordinary = portions_of(count, rows * top, most, lean, True), portions_of(count, rows * top, most, lean, False)
    places = jnp.arange(count)

    def named(tallies, turn):
        used = int((tallies > 0).sum())
        fixed = max(1, used // 4)
        shifted = fixed + (places - fixed + turn * (used - fixed)) % max(1, count - fixed)
        return jnp.zeros((count,), jnp.int32).at[ranking[jnp.where(places < fixed, places, shifted)]].set(jnp.asarray(tallies, jnp.int32))

    tallies = jnp.where(number % 4 == 0, named(crowded, number // 4), named(ordinary, number - number // 4 - 1))
    mixed = jax.random.permutation(jax.random.fold_in(own, 3), count)
    donor, receiver = mixed[0:count // 2 * 2:2], mixed[1:count // 2 * 2:2]
    slack = jnp.minimum(tallies[donor] - 1, most - tallies[receiver]) // 2
    slack = jnp.where((donor == ranking[0]) | (receiver == ranking[0]) | (tallies[receiver] == 0), 0, jnp.maximum(slack, 0))
    shifted = jax.random.randint(jax.random.fold_in(own, 4), (count // 2,), 0, 1 << 20) % (slack + 1)
    tallies = tallies.at[donor].add(-shifted).at[receiver].add(shifted)
    items = jnp.searchsorted(jnp.cumsum(tallies), jnp.arange(rows * top), side="right").astype(jnp.int32)
    grid = items.reshape(top, rows).T
    grid = grid[jax.random.permutation(jax.random.fold_in(own, 1), rows)]
    turn = jax.random.randint(jax.random.fold_in(own, 2), (rows, 1), 0, top)
    return jnp.take_along_axis(grid, (jnp.arange(top)[None, :] + turn) % top, axis=1)


def portions_of(count, total, limit, slope, full):
    portions = [(1 << 20) // math.isqrt(grade ** slope) + 1 for grade in range(1, count + 1)]
    largest = limit if full else min(limit, max(-(-total // count), total * portions[0] // sum(portions)))
    least = 1 if total - largest >= count - 1 else 0
    holding, rest = [largest] + [least] * (count - 1), total - largest - least * (count - 1)
    while rest > 0:
        candidates = [i for i in range(1, count) if holding[i] < largest] or [i for i in range(1, count) if holding[i] < limit]
        pool, remaining = sum([portions[i] for i in candidates]), rest
        for i in candidates:
            more = min(limit - holding[i], max(1, remaining * portions[i] // pool), rest)
            holding[i] = holding[i] + more
            rest = rest - more
    return np.array(holding)


def scatter_about(own_key, extent, width, reach, shards=(), kind=jnp.bfloat16):
    factor_of = steps_of(own_key, extent, shards, -0.22, 0.18) if shards else 1.0
    result = jax.random.normal(own_key, extent, jnp.float32) * width * factor_of
    return jnp.minimum(jnp.maximum(result, -reach), reach).astype(kind)


def setup_inputs(seed: int = 0, part: int = 0) -> dict:
    key_of = jax.random.split(jax.random.key(seed), 11)
    own_keys = jax.random.split(jax.random.fold_in(key_of[10], part), 11)
    tokens = scatter_about(own_keys[0], (TOKENS, D), 1.0, 6.0, ((0, 4),))
    expert_ids_keys = jax.random.split(jax.random.fold_in(own_keys[1], 1), TOKENS // TOK_DP)
    expert_ids_turns = jax.random.permutation(jax.random.fold_in(own_keys[1], 3), TOKENS // TOK_DP)
    expert_ids = jax.vmap(lambda own, number: assign_block(jax.random.fold_in(own_keys[1], 2), own, number, TOK_DP, EXPERTS, TOP, CAP, 2))(expert_ids_keys, expert_ids_turns).reshape((TOKENS, TOP))
    route_gates = jnp.clip(0.05 + 0.45 * jax.random.uniform(own_keys[2], (TOKENS, TOP), jnp.float32) ** steps_of(own_keys[2], (TOKENS, TOP), ((0, 4),), -0.2, 0.2), 0.05, 0.5)
    shared_gate_vec = scatter_about(key_of[3], (D,), D ** -0.5, 0.125)
    w_shared_gate = scatter_about(key_of[4], (D, FF_S), D ** -0.5, 0.125, ((0, 4), (1, 4)))
    w_shared_up = scatter_about(key_of[5], (D, FF_S), D ** -0.5, 0.125, ((0, 4), (1, 4)))
    w_shared_down_t = scatter_about(key_of[6], (D, FF_S), FF_S ** -0.5, 0.0625, ((0, 4), (1, 4)))
    w_expert_gate_t = scatter_about(key_of[7], (EXPERTS, FF_E, D), D ** -0.5, 0.125, ((0, 4), (1, 4)))
    w_expert_up_t = scatter_about(key_of[8], (EXPERTS, FF_E, D), D ** -0.5, 0.125, ((0, 4), (1, 4)))
    w_expert_down = scatter_about(key_of[9], (EXPERTS, FF_E, D), FF_E ** -0.5, 0.125, ((0, 4), (1, 4)))
    return {"tokens": tokens, "expert_ids": expert_ids, "route_gates": route_gates, "shared_gate_vec": shared_gate_vec, "w_shared_gate": w_shared_gate, "w_shared_up": w_shared_up, "w_shared_down_t": w_shared_down_t, "w_expert_gate_t": w_expert_gate_t, "w_expert_up_t": w_expert_up_t, "w_expert_down": w_expert_down}


def slot_places(expert_ids):
    blocks = expert_ids.reshape(N_DP, TOK_DP * TOP)
    labels = jnp.arange(EXPERTS, dtype=jnp.int32)
    onehot = (blocks[:, :, None] == labels[None, None, :]).astype(jnp.int32)
    before = jnp.cumsum(onehot, axis=1, dtype=jnp.int32) - onehot
    return jnp.sum(before * onehot, axis=2, dtype=jnp.int32).astype(jnp.int32)


def one_expert(operands):
    rows_in, w_gate, w_up, w_down = operands
    dims = (((1,), (1,)), ((), ()))
    gate_sum = lax.dot_general(rows_in, w_gate, dims, preferred_element_type=jnp.float32)
    up_sum = lax.dot_general(rows_in, w_up, dims, preferred_element_type=jnp.float32)
    hidden = (jax.nn.silu(gate_sum) * up_sum).astype(jnp.bfloat16)
    return jnp.dot(hidden, w_down, preferred_element_type=jnp.float32)


def reference(tokens, expert_ids, route_gates, shared_gate_vec, w_shared_gate, w_shared_up, w_shared_down_t, w_expert_gate_t, w_expert_up_t, w_expert_down):
    shared_gate = jnp.dot(tokens, w_shared_gate, preferred_element_type=jnp.float32)
    shared_up = jnp.dot(tokens, w_shared_up, preferred_element_type=jnp.float32)
    shared_hidden = (jax.nn.silu(shared_gate) * shared_up).astype(jnp.bfloat16)
    shared_out = lax.dot_general(shared_hidden, w_shared_down_t, (((1,), (1,)), ((), ())), preferred_element_type=jnp.float32)
    shared_scale = jax.nn.sigmoid(jnp.dot(tokens, shared_gate_vec, preferred_element_type=jnp.float32))
    places = slot_places(expert_ids).reshape(-1)
    flat_ids = expert_ids.reshape(-1).astype(jnp.int32)
    positions = jnp.arange(TOKENS * TOP, dtype=jnp.int32)
    block_index = positions // (TOK_DP * TOP)
    source_rows = positions // TOP
    target = (flat_ids * (N_DP * CAP) + block_index * CAP + places).astype(jnp.int32)
    buffer = jnp.zeros((EXPERTS * N_DP * CAP, D), jnp.bfloat16).at[target].set(tokens[source_rows])
    buffer = buffer.reshape(EXPERTS, N_DP * CAP, D)
    outputs = lax.map(one_expert, (buffer, w_expert_gate_t, w_expert_up_t, w_expert_down))
    picked = outputs.reshape(EXPERTS * N_DP * CAP, D)[target].reshape(TOKENS, TOP, D)
    routed = jnp.sum(picked * route_gates[:, :, None], axis=1)
    return (shared_scale[:, None] * shared_out + routed).astype(jnp.bfloat16)
```

```python
import jax
import jax.numpy as jnp
from jax import lax
from jax.sharding import PartitionSpec as P

CAP = 48
BF = jnp.bfloat16
F32 = jnp.float32
CHUNKS = 2


def slot_places(expert_ids, experts):
    flat_ids = expert_ids.reshape(-1)
    labels = jnp.arange(experts, dtype=jnp.int32)
    onehot = (flat_ids[:, None] == labels[None, :]).astype(jnp.int32)
    before = jnp.cumsum(onehot, axis=0, dtype=jnp.int32) - onehot
    return (jnp.sum(before * onehot, axis=1, dtype=jnp.int32), flat_ids)


def general(
    tokens,
    expert_ids,
    route_gates,
    shared_gate_vec,
    w_shared_gate,
    w_shared_up,
    w_shared_down_t,
    w_expert_gate_t,
    w_expert_up_t,
    w_expert_down,
):
    n_dp = lax.axis_size("dp")
    row_count, model_width = tokens.shape
    top_k = expert_ids.shape[1]
    exp_dev = w_expert_gate_t.shape[0]
    experts = exp_dev * n_dp
    portion_gate = lax.all_gather(w_shared_gate, "dp", axis=0, tiled=True)
    portion_up = lax.all_gather(w_shared_up, "dp", axis=0, tiled=True)
    portion_down = lax.all_gather(w_shared_down_t, "dp", axis=0, tiled=True)
    acc_gate = jnp.dot(tokens, portion_gate, preferred_element_type=jnp.float32)
    acc_up = jnp.dot(tokens, portion_up, preferred_element_type=jnp.float32)
    shared_hidden = (jax.nn.silu(acc_gate) * acc_up).astype(jnp.bfloat16)
    shared_part = lax.dot_general(
        shared_hidden, portion_down, (((1,), (1,)), ((), ())), preferred_element_type=jnp.float32
    )
    shared_scale = jax.nn.sigmoid(
        jnp.dot(tokens, shared_gate_vec, preferred_element_type=jnp.float32)
    )
    places, flat_ids = slot_places(expert_ids, experts)
    target = flat_ids * CAP + places
    source_rows = jnp.arange(row_count * top_k, dtype=jnp.int32) // top_k
    outgoing = (
        jnp.zeros((experts * CAP, model_width), jnp.bfloat16).at[target].set(tokens[source_rows])
    )
    arrived = lax.all_to_all(
        outgoing.reshape(n_dp, exp_dev * CAP, model_width),
        "dp",
        split_axis=0,
        concat_axis=0,
        tiled=True,
    )
    arrived = arrived.reshape(n_dp, exp_dev, CAP, model_width)
    ex_gate = jnp.einsum(
        "sjcd,jfd->sjcf", arrived, w_expert_gate_t, preferred_element_type=jnp.float32
    )
    ex_up = jnp.einsum("sjcd,jfd->sjcf", arrived, w_expert_up_t, preferred_element_type=jnp.float32)
    ex_hidden = (jax.nn.silu(ex_gate) * ex_up).astype(jnp.bfloat16)
    ex_part = jnp.einsum(
        "sjcf,jfd->sjcd", ex_hidden, w_expert_down, preferred_element_type=jnp.float32
    )
    returned = lax.all_to_all(
        ex_part.reshape(n_dp, exp_dev * CAP, model_width),
        "dp",
        split_axis=0,
        concat_axis=0,
        tiled=True,
    )
    returned = returned.reshape(experts * CAP, model_width)
    picked = returned[target].reshape(row_count, top_k, model_width)
    routed = jnp.sum(picked * route_gates[:, :, None], axis=1)
    combined = shared_scale[:, None] * shared_part + routed
    return lax.psum_scatter(combined, "tensor", scatter_dimension=1, tiled=True).astype(
        jnp.bfloat16
    )


def swap(x, axis, bit):
    n = lax.axis_size(axis)
    return lax.ppermute(x, axis, [(i, i ^ bit) for i in range(n)])


def pack_pair(first, second, start, side, width):
    rows = first.shape[0]
    whole = width - 64
    wide = start + side * (width + 64)
    mid = start + whole

    def part(m):
        body = lax.dynamic_slice(m, (0, wide), (rows, whole))
        tile = lax.dynamic_slice(m, (0, mid), (rows, 128))
        return body, jnp.where(side == 0, tile[:, :64], tile[:, 64:])

    body_a, half_a = part(first)
    body_b, half_b = part(second)
    return jnp.concatenate([body_a, half_a, half_b, body_b], axis=1)


def exchanged(
    tokens,
    expert_ids,
    route_gates,
    shared_gate_vec,
    w_shared_gate,
    w_shared_up,
    w_shared_down_t,
    w_expert_gate_t,
    w_expert_up_t,
    w_expert_down,
):
    z, t, g = lax.axis_index("dp"), lax.axis_index("tensor"), lax.axis_index("groups")
    n_dp, n_t, n_g = lax.axis_size("dp"), lax.axis_size("tensor"), lax.axis_size("groups")
    rows, d = tokens.shape
    e_dev, ff_e, _ = w_expert_gate_t.shape
    d_part, ff = w_shared_gate.shape
    width = ff // (n_dp * n_g)
    whole = width - 64
    step = d_part // CHUNKS
    half = step // 2

    gu_pieces, down_pieces = [], []
    for k in range(n_dp):
        start = (z ^ k) * (2 * width)
        gu_pieces.append(pack_pair(w_shared_gate, w_shared_up, start, g, width))
        down_pieces.append(
            [
                pack_pair(
                    w_shared_down_t[step * c : step * c + half],
                    w_shared_down_t[step * c + half : step * (c + 1)],
                    start,
                    g,
                    width,
                )
                for c in range(CHUNKS)
            ]
        )

    quarter = rows // n_t
    mine = lax.dynamic_slice(tokens, (t * quarter, 0), (quarter, d))
    over_z = jnp.stack([mine] + [swap(mine, "dp", k) for k in range(1, n_dp)])

    def spread(q):
        other = swap(q, "tensor", 2)
        q1, other1 = swap(q, "tensor", 1), swap(other, "tensor", 1)
        full = jnp.zeros((n_dp, n_t, quarter, d), BF)
        for piece, idx in ((q, t), (other, t ^ 2), (q1, t ^ 1), (other1, t ^ 3)):
            full = lax.dynamic_update_slice(full, piece[:, None], (0, idx, 0, 0))
        return full.reshape(n_dp * rows, d)

    tok_own = spread(over_z)
    tok_other = spread(swap(over_z, "groups", 1))

    def gates_for(owner):
        labels = owner * e_dev + jnp.arange(e_dev, dtype=jnp.int32)
        hit = expert_ids[None, :, :] == labels[:, None, None]
        return jnp.sum(jnp.where(hit, route_gates[None, :, :], 0.0), axis=2)

    gate_cols = [gates_for(z)] + [swap(gates_for(z ^ k), "dp", k) for k in range(1, n_dp)]
    gate_matrix = jnp.concatenate(gate_cols, axis=1)

    dims = (((1,), (1,)), ((), ()))
    eg = lax.dot_general(
        tok_own, w_expert_gate_t.reshape(e_dev * ff_e, d), dims, preferred_element_type=F32
    )
    eu = lax.dot_general(
        tok_own, w_expert_up_t.reshape(e_dev * ff_e, d), dims, preferred_element_type=F32
    )
    spread_gates = jnp.repeat(gate_matrix.T, ff_e, axis=1)
    eh = (jax.nn.silu(eg) * eu * spread_gates).astype(BF)
    routed = jnp.dot(eh, w_expert_down.reshape(e_dev * ff_e, d), preferred_element_type=F32)
    routed_t = routed.T

    gu = [gu_pieces[0]] + [swap(gu_pieces[k], "dp", k) for k in range(1, n_dp)]
    w_gu = jnp.zeros((n_dp * d_part, 2 * width), BF)
    for k in range(n_dp):
        w_gu = lax.dynamic_update_slice(w_gu, gu[k], ((z ^ k) * d_part, 0))
    tok_all = jnp.concatenate([tok_own, tok_other], axis=0)
    acc = jnp.dot(tok_all, w_gu, preferred_element_type=F32)
    s_gate, s_up = acc[:, :width], jnp.concatenate([acc[:, width + 64 :], acc[:, width : width + 64]], 1)
    s_hidden = (jax.nn.silu(s_gate) * s_up).astype(BF)
    zero = jnp.zeros_like(s_hidden)
    left = jnp.concatenate([s_hidden, zero], axis=1)
    right = jnp.concatenate([zero[:, :width], s_hidden[:, whole:], s_hidden[:, :whole]], axis=1)
    scale = jax.nn.sigmoid(
        lax.dot_general(
            shared_gate_vec[None, :], tok_all, dims, preferred_element_type=F32
        )
    )
    n_tok = n_dp * rows

    routed_blocks = routed_t.reshape(n_t, d // n_t, n_tok)
    out_rows = []
    for c in range(CHUNKS):
        wd = [down_pieces[0][c]] + [swap(down_pieces[k][c], "dp", k) for k in range(1, n_dp)]
        w_d = jnp.zeros((n_dp, half, 2 * width), BF)
        for k in range(n_dp):
            w_d = lax.dynamic_update_slice(w_d, wd[k][None], (z ^ k, 0, 0))
        w_d = w_d.reshape(n_dp * half, 2 * width)
        top = lax.dot_general(w_d, left, dims, preferred_element_type=F32)
        bottom = lax.dot_general(w_d, right, dims, preferred_element_type=F32)
        part = jnp.concatenate(
            [top.reshape(n_dp, half, -1), bottom.reshape(n_dp, half, -1)], axis=1
        )
        part = part * scale
        own = part[:, :, :n_tok] + routed_blocks[:, step * c : step * (c + 1), :]
        part = jnp.concatenate([own, part[:, :, n_tok:]], axis=2)
        pairs = part.reshape(n_t // 2, 2, step, 2 * n_tok)
        keep = lax.dynamic_index_in_dim(pairs, t & 1, 1, keepdims=False)
        give = lax.dynamic_index_in_dim(pairs, (t & 1) ^ 1, 1, keepdims=False).astype(BF)
        keep = keep + swap(give, "tensor", 1).astype(F32)
        here = lax.dynamic_index_in_dim(keep, t >> 1, 0, keepdims=False)
        there = lax.dynamic_index_in_dim(keep, (t >> 1) ^ 1, 0, keepdims=False).astype(BF)
        total = here[:, :n_tok] + swap(there[:, :n_tok], "tensor", 2).astype(F32)
        total = total + swap(here[:, n_tok:].astype(BF), "groups", 1).astype(F32)
        far = there[:, n_tok:]
        n_pair = n_g * n_t
        total = total + lax.ppermute(
            far, ("groups", "tensor"), [(i, i ^ (n_t + 2)) for i in range(n_pair)]
        ).astype(F32)
        done = total[:, :rows]
        for k in range(1, n_dp):
            piece = total[:, rows * k : rows * (k + 1)].astype(BF)
            done = done + swap(piece, "dp", k).astype(F32)
        out_rows.append(done)
    return jnp.concatenate(out_rows, axis=0).T.astype(BF)


def solution(mesh):
    sizes = mesh.shape

    def on_device(*args):
        d_part, ff = args[4].shape
        width = ff // (sizes["dp"] * sizes["groups"])
        fits = (
            sizes["dp"] == 4
            and sizes["tensor"] == 4
            and sizes["groups"] == 2
            and width % 128 == 64
            and d_part % (32 * CHUNKS) == 0
            and args[0].shape[0] % 128 == 0
        )
        return (exchanged if fits else general)(*args)

    return jax.shard_map(
        on_device,
        mesh=mesh,
        in_specs=(
            P(("groups", "dp"), None),
            P(("groups", "dp"), None),
            P(("groups", "dp"), None),
            P(),
            P("dp", "tensor"),
            P("dp", "tensor"),
            P("dp", "tensor"),
            P("dp", "tensor", None),
            P("dp", "tensor", None),
            P("dp", "tensor", None),
        ),
        out_specs=P(("groups", "dp"), "tensor"),
        check_vma=False,
    )
```

```python
import jax
import jax.numpy as jnp
from jax import lax
from jax.experimental import pallas as pl
from jax.experimental.pallas import tpu as pltpu
from jax.sharding import PartitionSpec as P

CAP = 48
BF = jnp.bfloat16
F32 = jnp.float32


def slot_places(expert_ids, experts):
    flat_ids = expert_ids.reshape(-1)
    labels = jnp.arange(experts, dtype=jnp.int32)
    onehot = (flat_ids[:, None] == labels[None, :]).astype(jnp.int32)
    before = jnp.cumsum(onehot, axis=0, dtype=jnp.int32) - onehot
    return (jnp.sum(before * onehot, axis=1, dtype=jnp.int32), flat_ids)


def general(
    tokens,
    expert_ids,
    route_gates,
    shared_gate_vec,
    w_shared_gate,
    w_shared_up,
    w_shared_down_t,
    w_expert_gate_t,
    w_expert_up_t,
    w_expert_down,
):
    n_dp = lax.axis_size("dp")
    row_count, model_width = tokens.shape
    top_k = expert_ids.shape[1]
    exp_dev = w_expert_gate_t.shape[0]
    experts = exp_dev * n_dp
    portion_gate = lax.all_gather(w_shared_gate, "dp", axis=0, tiled=True)
    portion_up = lax.all_gather(w_shared_up, "dp", axis=0, tiled=True)
    portion_down = lax.all_gather(w_shared_down_t, "dp", axis=0, tiled=True)
    acc_gate = jnp.dot(tokens, portion_gate, preferred_element_type=jnp.float32)
    acc_up = jnp.dot(tokens, portion_up, preferred_element_type=jnp.float32)
    shared_hidden = (jax.nn.silu(acc_gate) * acc_up).astype(jnp.bfloat16)
    shared_part = lax.dot_general(
        shared_hidden, portion_down, (((1,), (1,)), ((), ())), preferred_element_type=jnp.float32
    )
    shared_scale = jax.nn.sigmoid(
        jnp.dot(tokens, shared_gate_vec, preferred_element_type=jnp.float32)
    )
    places, flat_ids = slot_places(expert_ids, experts)
    target = flat_ids * CAP + places
    source_rows = jnp.arange(row_count * top_k, dtype=jnp.int32) // top_k
    outgoing = (
        jnp.zeros((experts * CAP, model_width), jnp.bfloat16).at[target].set(tokens[source_rows])
    )
    arrived = lax.all_to_all(
        outgoing.reshape(n_dp, exp_dev * CAP, model_width),
        "dp",
        split_axis=0,
        concat_axis=0,
        tiled=True,
    )
    arrived = arrived.reshape(n_dp, exp_dev, CAP, model_width)
    ex_gate = jnp.einsum(
        "sjcd,jfd->sjcf", arrived, w_expert_gate_t, preferred_element_type=jnp.float32
    )
    ex_up = jnp.einsum("sjcd,jfd->sjcf", arrived, w_expert_up_t, preferred_element_type=jnp.float32)
    ex_hidden = (jax.nn.silu(ex_gate) * ex_up).astype(jnp.bfloat16)
    ex_part = jnp.einsum(
        "sjcf,jfd->sjcd", ex_hidden, w_expert_down, preferred_element_type=jnp.float32
    )
    returned = lax.all_to_all(
        ex_part.reshape(n_dp, exp_dev * CAP, model_width),
        "dp",
        split_axis=0,
        concat_axis=0,
        tiled=True,
    )
    returned = returned.reshape(experts * CAP, model_width)
    picked = returned[target].reshape(row_count, top_k, model_width)
    routed = jnp.sum(picked * route_gates[:, :, None], axis=1)
    combined = shared_scale[:, None] * shared_part + routed
    return lax.psum_scatter(combined, "tensor", scatter_dimension=1, tiled=True).astype(
        jnp.bfloat16
    )


def swap(x, axis, bit):
    n = lax.axis_size(axis)
    return lax.ppermute(x, axis, [(i, i ^ bit) for i in range(n)])


def vmem_full(a):
    return pl.BlockSpec(a.shape, lambda *_: (0,) * a.ndim)


ANY = pl.BlockSpec(memory_space=pl.ANY)
FULL = 60 << 20
SMEM = pl.BlockSpec(memory_space=pltpu.SMEM)


def run_all(copies):
    for c in copies:
        c.start()
    for c in copies:
        c.wait()


def token_rows(where, tokens, ids_t, gates_t):
    rows, d = tokens.shape
    top = ids_t.shape[0]
    quarter = rows // 4

    def kernel(where_ref, tok_ref, ids_ref, gates_ref, mine, tags, sem):
        at = pl.multiple_of(where_ref[1] * quarter, quarter)
        copy = pltpu.make_async_copy(
            tok_ref.at[pl.ds(at, quarter)], mine.at[:, pl.ds(0, d)], sem
        )
        copy.start()
        gates = gates_ref[...]
        high = gates.astype(BF).astype(F32)
        lines = [ids_ref[...].astype(F32), high, gates - high]
        lines.append(jnp.zeros((128 - 3 * top, rows), F32))
        tags[...] = jnp.concatenate(lines, axis=0).T
        mine[:, pl.ds(d, 128)] = tags[pl.ds(at, quarter), :].astype(BF)
        copy.wait()

    vm = pl.BlockSpec(memory_space=pltpu.VMEM)
    return pl.pallas_call(
        kernel,
        out_shape=jax.ShapeDtypeStruct((quarter, d + 128), BF),
        in_specs=[SMEM, ANY, vm, vm],
        out_specs=vm,
        scratch_shapes=[pltpu.VMEM((rows, 128), F32), pltpu.SemaphoreType.DMA],
        compiler_params=pltpu.CompilerParams(vmem_limit_bytes=FULL),
        name="token_rows",
    )(where, tokens, ids_t, gates_t)


def pack(where, wg, wu, wd, width):
    d_part, ff = wg.shape
    n = ff // (2 * width)
    whole = width - 64
    half = d_part // 2

    def kernel(where_ref, g_ref, u_ref, d_ref, *rest):
        outs_gu, outs_d = rest[:n], rest[n : 2 * n]
        gu_buf, d_buf, gu_mid, d_mid, in_sem, out_sem = rest[2 * n :]
        z, t, g = where_ref[0], where_ref[1], where_ref[2]
        side = g * (width + 64)
        loads = []
        for k in range(n):
            start = (z ^ k) * (2 * width)
            wide = pl.multiple_of(start + side, 128)
            mid = pl.multiple_of(start + whole, 128)
            jobs = []
            for m, ref in enumerate((g_ref, u_ref)):
                lane = 0 if m == 0 else width + 64
                jobs.append((ref.at[:, pl.ds(wide, whole)], gu_buf.at[k, :, pl.ds(lane, whole)]))
                jobs.append((ref.at[:, pl.ds(mid, 128)], gu_mid.at[k, m]))
            loads.append(jobs)
        for r in range(n):
            start = (t ^ r) * (2 * width)
            wide = pl.multiple_of(start + side, 128)
            mid = pl.multiple_of(start + whole, 128)
            jobs = []
            for m in range(2):
                lane = 0 if m == 0 else width + 64
                part = d_ref.at[pl.ds(m * half, half)]
                jobs.append((part.at[:, pl.ds(wide, whole)], d_buf.at[r, :, pl.ds(lane, whole)]))
                jobs.append((part.at[:, pl.ds(mid, 128)], d_mid.at[r, m]))
            loads.append(jobs)
        order = [1, 2, 3, 0, n, n + 1, n + 2, n + 3]
        copies = {}
        for i in order:
            copies[i] = [
                pltpu.make_async_copy(s, d, in_sem.at[i, j]) for j, (s, d) in enumerate(loads[i])
            ]
            for c in copies[i]:
                c.start()
        stores = []
        for i in order:
            for c in copies[i]:
                c.wait()
            buf, mids, out = (gu_buf, gu_mid, outs_gu[i]) if i < n else (d_buf, d_mid, outs_d[i - n])
            p = i % n
            first = pltpu.roll(mids[p, 0].astype(F32), 64 * g, 1)
            second = pltpu.roll(mids[p, 1].astype(F32), 64 * (1 - g), 1)
            lane = lax.broadcasted_iota(jnp.int32, first.shape, 1)
            buf[p, :, pl.ds(whole, 128)] = jnp.where(lane < 64, first, second).astype(BF)
            stores.append(pltpu.make_async_copy(buf.at[p], out, out_sem.at[i]))
            stores[-1].start()
        for c in stores:
            c.wait()

    return pl.pallas_call(
        kernel,
        out_shape=[jax.ShapeDtypeStruct((d_part, 2 * width), BF)] * n
        + [jax.ShapeDtypeStruct((half, 2 * width), BF)] * n,
        in_specs=[SMEM, ANY, ANY, ANY],
        out_specs=[ANY] * (2 * n),
        scratch_shapes=[
            pltpu.VMEM((n, d_part, 2 * width), BF),
            pltpu.VMEM((n, half, 2 * width), BF),
            pltpu.VMEM((n, 2, d_part, 128), BF),
            pltpu.VMEM((n, 2, half, 128), BF),
            pltpu.SemaphoreType.DMA((2 * n, 4)),
            pltpu.SemaphoreType.DMA((2 * n,)),
        ],
        compiler_params=pltpu.CompilerParams(vmem_limit_bytes=FULL),
        cost_estimate=pl.CostEstimate(flops=0, bytes_accessed=8 << 20, transcendentals=0),
        name="pack",
    )(where, wg, wu, wd)


def token_copies(where_ref, direct, crossed, rows_ref, info_ref, sem, base):
    t = where_ref[1]
    _, n_dp, quarter, _ = direct.shape
    d = rows_ref.shape[1]
    copies = []
    for b, ref in ((0, direct), (2, direct), (1, crossed), (3, crossed)):
        for k in range(n_dp):
            row = pl.multiple_of(base + k * 4 * quarter + (t ^ b) * quarter, quarter)
            src = ref.at[b // 2, k]
            copies.append(
                pltpu.make_async_copy(
                    src.at[:, pl.ds(0, d)], rows_ref.at[pl.ds(row, quarter)], sem.at[len(copies)]
                )
            )
            if info_ref is not None:
                copies.append(
                    pltpu.make_async_copy(
                        src.at[:, pl.ds(d, 128)],
                        info_ref.at[pl.ds(row, quarter)],
                        sem.at[len(copies)],
                    )
                )
    return copies


def routed_experts(where, direct, crossed, eg, eu, ed, top):
    e_dev, ff_e, d = eg.shape
    n_dp = direct.shape[1]
    n_tok = n_dp * direct.shape[2] * 4
    slots = n_dp * CAP
    part = d // 4

    def kernel(
        where_ref, dir_ref, cro_ref, g_ref, u_ref, w_ref, give, keep,
        tok, info, place_t, gate_t, back, outs, acc_t, sem,
    ):
        e = pl.program_id(0)
        z, t = where_ref[0], where_ref[1]

        @pl.when(e == 0)
        def _():
            run_all(token_copies(where_ref, dir_ref, cro_ref, tok, info, sem, 0))
            tags = info[...].astype(F32)
            lane = lax.broadcasted_iota(jnp.int32, tags.shape, 1)
            weight = pltpu.roll(tags, 128 - top, 1) + pltpu.roll(tags, 128 - 2 * top, 1)
            chosen = jnp.zeros(tags.shape, F32)
            gates = jnp.zeros(tags.shape, F32)
            for i in range(e_dev):
                hit = (tags == (z * e_dev + i).astype(F32)) & (lane < top)
                has = jnp.sum(jnp.where(hit, 1.0, 0.0), axis=1, keepdims=True)
                gate = jnp.sum(jnp.where(hit, weight, 0.0), axis=1, keepdims=True)
                chosen = jnp.where(lane == i, has, chosen)
                gates = jnp.where(lane == i, gate, gates)
            row = lax.broadcasted_iota(jnp.int32, (n_tok, n_tok), 0)
            col = lax.broadcasted_iota(jnp.int32, (n_tok, n_tok), 1)
            earlier = jnp.where(col < row, 1.0, 0.0).astype(BF)
            before = jnp.dot(earlier, chosen.astype(BF), preferred_element_type=F32)
            where_to = jnp.where(chosen > 0.5, before, -1.0)
            place_t[...] = where_to.T
            gate_t[...] = gates.T

        line = place_t[pl.ds(e, 1), :]
        slot = lax.broadcasted_iota(jnp.int32, (slots, n_tok), 0).astype(F32)
        hit = slot == line
        pick = jnp.where(hit, 1.0, 0.0).astype(BF)
        gate_of = jnp.sum(jnp.where(hit, gate_t[pl.ds(e, 1), :], 0.0), axis=1, keepdims=True)
        x = jnp.dot(pick, tok[...], preferred_element_type=F32).astype(BF)
        dims = (((1,), (1,)), ((), ()))
        gate = lax.dot_general(x, g_ref[0], dims, preferred_element_type=F32)
        up = lax.dot_general(x, u_ref[0], dims, preferred_element_type=F32)
        hidden = (gate * jax.nn.sigmoid(gate) * up).astype(BF)
        out = jnp.dot(hidden, w_ref[0], preferred_element_type=F32)
        at = pl.multiple_of(e * slots, slots)
        outs[pl.ds(at, slots), :] = (gate_of * out).astype(BF)
        back[pl.ds(at, slots), :] = pick

        @pl.when(e == e_dev - 1)
        def _():
            dims = (((0,), (0,)), ((), ()))
            for i in range(d // 256):
                acc_t[pl.ds(256 * i, 256), :] = lax.dot_general(
                    outs[:, pl.ds(256 * i, 256)], back[...], dims, preferred_element_type=F32
                )
            for b in range(2):
                mine = pl.multiple_of((t ^ (2 * b)) * part, part)
                theirs = pl.multiple_of((t ^ (2 * b + 1)) * part, part)
                keep[b] = acc_t[pl.ds(mine, part), :]
                give[b] = acc_t[pl.ds(theirs, part), :].astype(BF)

    weights = pl.BlockSpec((1, ff_e, d), lambda e: (e, 0, 0))
    n_copies = 2 * 4 * n_dp
    return pl.pallas_call(
        kernel,
        grid=(e_dev,),
        out_shape=[
            jax.ShapeDtypeStruct((2, part, n_tok), BF),
            jax.ShapeDtypeStruct((2, part, n_tok), F32),
        ],
        in_specs=[SMEM, ANY, ANY, weights, weights, weights],
        out_specs=[
            pl.BlockSpec((2, part, n_tok), lambda e: (0, 0, 0)),
            pl.BlockSpec((2, part, n_tok), lambda e: (0, 0, 0)),
        ],
        scratch_shapes=[
            pltpu.VMEM((n_tok, d), BF),
            pltpu.VMEM((n_tok, 128), BF),
            pltpu.VMEM((128, n_tok), F32),
            pltpu.VMEM((128, n_tok), F32),
            pltpu.VMEM((e_dev * slots, n_tok), BF),
            pltpu.VMEM((e_dev * slots, d), BF),
            pltpu.VMEM((d, n_tok), F32),
            pltpu.SemaphoreType.DMA((n_copies,)),
        ],
        compiler_params=pltpu.CompilerParams(vmem_limit_bytes=52 << 20),
        cost_estimate=pl.CostEstimate(
            flops=6 * slots * e_dev * ff_e * d + 4 * slots * e_dev * n_tok * d,
            bytes_accessed=6 * e_dev * ff_e * d,
            transcendentals=slots * e_dev * ff_e,
        ),
        name="routed",
    )(where, direct, crossed, eg, eu, ed)


def shared_hidden(where, own, other, pieces, vec, after, width):
    d_part = pieces[0].shape[0]
    n = len(pieces)
    d = n * d_part
    n_tok = own[0].shape[1] * own[0].shape[2] * 4
    whole = width - 64

    def kernel(where_ref, a0, a1, b0, b1, vec_ref, *rest):
        p_refs = rest[:n]
        hid, scale, tok, w, tok_sem, w_sem = rest[n + 1 :]
        z = where_ref[0]
        t_copies = token_copies(where_ref, a0, a1, tok, None, tok_sem.at[0], 0)
        t_copies += token_copies(where_ref, b0, b1, tok, None, tok_sem.at[1], n_tok)
        w_copies = []
        for k in range(n):
            row = pl.multiple_of((z ^ k) * d_part, d_part)
            w_copies.append(
                pltpu.make_async_copy(p_refs[k], w.at[pl.ds(row, d_part)], w_sem.at[k])
            )
        run_all(w_copies + t_copies)
        dims = (((1,), (1,)), ((), ()))
        lines = jnp.broadcast_to(vec_ref[...], (8, d))
        def half_hidden(row):
            x = tok[pl.ds(row, 256), :]
            acc = jnp.dot(x, w[...], preferred_element_type=F32)
            gate_mid = acc[:, whole : whole + 128]
            up_mid = pltpu.roll(gate_mid, 64, 1)
            gate, up = acc[:, :whole], acc[:, width + 64 :]
            line = lax.dot_general(lines, x, dims, preferred_element_type=F32)
            scale[:, pl.ds(row, 256)] = jax.nn.sigmoid(line[:1])
            body = gate * jax.nn.sigmoid(gate) * up
            return body.astype(BF), gate_mid * jax.nn.sigmoid(gate_mid) * up_mid

        for row in range(0, n_tok, 256):
            rows = pl.ds(row, 256)
            body, mid = half_hidden(row)
            far_body, far_mid = half_hidden(n_tok + row)
            lane = lax.broadcasted_iota(jnp.int32, mid.shape, 1)
            hid[rows, pl.ds(0, whole)] = body
            hid[rows, pl.ds(width + 64, whole)] = far_body
            mid = jnp.where(lane < 64, mid, pltpu.roll(far_mid, 64, 1))
            hid[rows, pl.ds(whole, 128)] = mid.astype(BF)

    return pl.pallas_call(
        kernel,
        out_shape=[
            jax.ShapeDtypeStruct((n_tok, 2 * width), BF),
            jax.ShapeDtypeStruct((1, 2 * n_tok), F32),
        ],
        in_specs=[SMEM] + [ANY] * 4 + [pl.BlockSpec(memory_space=pltpu.VMEM)] + [ANY] * (n + 1),
        out_specs=[pl.BlockSpec(memory_space=pltpu.VMEM)] * 2,
        scratch_shapes=[
            pltpu.VMEM((2 * n_tok, d), BF),
            pltpu.VMEM((d, 2 * width), BF),
            pltpu.SemaphoreType.DMA((2, 4 * own[0].shape[1])),
            pltpu.SemaphoreType.DMA((n,)),
        ],
        compiler_params=pltpu.CompilerParams(vmem_limit_bytes=24 << 20),
        cost_estimate=pl.CostEstimate(
            flops=2 * 2 * n_tok * d * 2 * width,
            bytes_accessed=8 << 20,
            transcendentals=2 * n_tok * width,
        ),
        name="shared_hidden",
    )(where, own[0], own[1], other[0], other[1], vec, *pieces, after)


def shared_down(where, pieces, direct, crossed, scale, routed, width):
    n = len(pieces)
    half = pieces[0].shape[0]
    whole = width - 64
    lanes = whole + 128
    n_tok = direct.shape[1]
    both = 2 * n_tok

    def kernel(where_ref, dir_ref, cro_ref, scale_ref, routed_ref, *rest):
        p_refs = rest[:n]
        far, near, w, h, w_sem, h_sem = rest[n:]
        z, t = where_ref[0], where_ref[1]
        copies = []
        for r in range(n):
            jobs = (
                (p_refs[r].at[:, pl.ds(0, lanes)], w.at[pl.ds(0, half), pl.ds(lanes * r, lanes)]),
                (
                    p_refs[r].at[:, pl.ds(lanes, whole)],
                    w.at[pl.ds(half, half), pl.ds(lanes * r, whole)],
                ),
                (
                    p_refs[r].at[:, pl.ds(whole, 128)],
                    w.at[pl.ds(half, half), pl.ds(lanes * r + whole, 128)],
                ),
            )
            for j, (s, d) in enumerate(jobs):
                copies.append(pltpu.make_async_copy(s, d, w_sem.at[r, j]))
        for m, ref in ((0, dir_ref), (2, dir_ref), (1, cro_ref), (3, cro_ref)):
            at = pl.multiple_of((z ^ t ^ m) * lanes, lanes)
            src = ref.at[m // 2]
            jobs = (
                (src.at[:, pl.ds(0, lanes)], h.at[pl.ds(0, n_tok), pl.ds(at, lanes)]),
                (
                    src.at[:, pl.ds(lanes, whole)],
                    h.at[pl.ds(n_tok, n_tok), pl.ds(at, whole)],
                ),
                (
                    src.at[:, pl.ds(whole, 128)],
                    h.at[pl.ds(n_tok, n_tok), pl.ds(at + whole, 128)],
                ),
            )
            for j, (s, d) in enumerate(jobs):
                copies.append(pltpu.make_async_copy(s, d, h_sem.at[m, j]))
        run_all(copies)
        lane = lax.broadcasted_iota(jnp.int32, (half, 128), 1)
        for r in range(n):
            at = pl.ds(lanes * r + whole, 128)
            for i, mask in ((0, lane < 64), (1, lane >= 64)):
                rows = pl.ds(half * i, half)
                w[rows, at] = jnp.where(mask, w[rows, at].astype(F32), 0.0).astype(BF)
        lane = lax.broadcasted_iota(jnp.int32, (n_tok, 128), 1)
        for r in range(n):
            at = pl.ds(lanes * r + whole, 128)
            for i, own in ((0, lane < 64), (1, lane >= 64)):
                rows = pl.ds(n_tok * i, n_tok)
                mid = h[rows, at].astype(F32)
                h[rows, at] = jnp.where(own, mid, pltpu.roll(mid, 64, 1)).astype(BF)
        dims = (((1,), (1,)), ((), ()))
        out = lax.dot_general(w[...], h[pl.ds(n_tok, n_tok), :], dims, preferred_element_type=F32)
        far[...] = (out * scale_ref[:, pl.ds(n_tok, n_tok)]).astype(BF)
        out = lax.dot_general(w[...], h[pl.ds(0, n_tok), :], dims, preferred_element_type=F32)
        near[...] = out * scale_ref[:, pl.ds(0, n_tok)] + routed_ref[...]

    vm = pl.BlockSpec(memory_space=pltpu.VMEM)
    return pl.pallas_call(
        kernel,
        out_shape=[
            jax.ShapeDtypeStruct((2 * half, n_tok), BF),
            jax.ShapeDtypeStruct((2 * half, n_tok), F32),
        ],
        in_specs=[SMEM, ANY, ANY, vm, vm] + [ANY] * n,
        out_specs=[vm, vm],
        scratch_shapes=[
            pltpu.VMEM((2 * half, n * lanes), BF),
            pltpu.VMEM((both, n * lanes), BF),
            pltpu.SemaphoreType.DMA((n, 3)),
            pltpu.SemaphoreType.DMA((4, 3)),
        ],
        compiler_params=pltpu.CompilerParams(vmem_limit_bytes=24 << 20),
        cost_estimate=pl.CostEstimate(
            flops=2 * 2 * half * n * lanes * both, bytes_accessed=6 << 20, transcendentals=0
        ),
        name="shared_down",
    )(where, direct, crossed, scale, routed, *pieces)


def exchanged(
    tokens,
    expert_ids,
    route_gates,
    shared_gate_vec,
    w_shared_gate,
    w_shared_up,
    w_shared_down_t,
    w_expert_gate_t,
    w_expert_up_t,
    w_expert_down,
):
    z, t, g = lax.axis_index("dp"), lax.axis_index("tensor"), lax.axis_index("groups")
    n_dp, n_t, n_g = lax.axis_size("dp"), lax.axis_size("tensor"), lax.axis_size("groups")
    where = jnp.stack([z, t, g]).astype(jnp.int32)
    rows, d = tokens.shape
    top = expert_ids.shape[1]
    width = w_shared_gate.shape[1] // (n_dp * n_g)

    some = expert_ids[0, 0] >= 0

    def apart(step, *operands):
        shapes = jax.eval_shape(step, *operands)
        empty = lambda *_: jax.tree.map(lambda a: jnp.zeros(a.shape, a.dtype), shapes)
        return lax.cond(some, step, empty, *operands)

    def first_step(mine, *weights):
        packed = pack(where, *weights, width)
        over_z = jnp.stack([mine] + [swap(mine, "dp", k) for k in range(1, n_dp)])
        return over_z, packed

    over_z, packed = apart(
        first_step,
        token_rows(where, tokens, expert_ids.T, route_gates.T),
        w_shared_gate,
        w_shared_up,
        w_shared_down_t,
    )
    gu = [packed[0]] + [swap(packed[k], "dp", k) for k in range(1, n_dp)]

    def spread(q):
        direct = jnp.stack([q, swap(q, "tensor", 2)])
        return direct, swap(direct, "tensor", 1)

    def cross(piece, r):
        route = [(i * n_t + j, (j ^ r) * n_t + i) for i in range(n_dp) for j in range(n_t)]
        return lax.ppermute(piece, ("dp", "tensor"), route)

    def routed_step(q, piece, *weights):
        direct = jnp.stack([q, swap(q, "tensor", 2)])
        direct, other = lax.optimization_barrier((direct, swap(q, "groups", 1)))
        crossed, other = lax.optimization_barrier((swap(direct, "tensor", 1), other))
        over_x = swap(other, "tensor", 2)
        piece = cross(piece, 0)
        give, keep = routed_experts(where, direct, crossed, *weights, top)
        other, over_x, give, piece = lax.optimization_barrier((other, over_x, give, piece))
        other = jnp.stack([other, over_x])
        return (direct, crossed), (other, swap(other, "tensor", 1)), give, keep, piece

    tok_own, tok_other, give, keep, first = apart(
        routed_step, over_z, packed[n_dp], w_expert_gate_t, w_expert_up_t, w_expert_down
    )
    hidden, scale = shared_hidden(
        where, tok_own, tok_other, gu, shared_gate_vec[None, :], give, width
    )

    def gather_step(h, out, kept):
        got = swap(out, "tensor", 1).astype(F32)
        return spread(h), kept[0] + got[0], (kept[1] + got[1]).astype(BF)

    (h_direct, h_crossed), routed, routed_far = apart(gather_step, hidden, give, keep)

    down = [first] + [cross(packed[n_dp + r], r) for r in range(1, n_dp)]
    far, near = shared_down(where, down, h_direct, h_crossed, scale, routed, width)
    total = near + swap(far, "groups", 1).astype(F32) + swap(routed_far, "tensor", 2).astype(F32)
    done = total[:, :rows]
    for k in range(1, n_dp):
        piece = total[:, rows * k : rows * (k + 1)].astype(BF)
        done = done + swap(piece, "dp", k).astype(F32)
    return done.T.astype(BF)


def solution(mesh):
    sizes = mesh.shape

    def on_device(*args):
        d_part, ff = args[4].shape
        width = ff // (sizes["dp"] * sizes["groups"])
        fits = (
            sizes["dp"] == 4
            and sizes["tensor"] == 4
            and sizes["groups"] == 2
            and width % 128 == 64
            and d_part % 32 == 0
            and args[7].shape[2] % 256 == 0
            and args[1].shape[1] == 8
            and args[0].shape[0] % 128 == 0
        )
        return (exchanged if fits else general)(*args)

    return jax.shard_map(
        on_device,
        mesh=mesh,
        in_specs=(
            P(("groups", "dp"), None),
            P(("groups", "dp"), None),
            P(("groups", "dp"), None),
            P(),
            P("dp", "tensor"),
            P("dp", "tensor"),
            P("dp", "tensor"),
            P("dp", "tensor", None),
            P("dp", "tensor", None),
            P("dp", "tensor", None),
        ),
        out_specs=P(("groups", "dp"), "tensor"),
        check_vma=False,
    )
```

```python
import jax
import jax.numpy as jnp
from jax import lax
from jax.experimental import pallas as pl
from jax.experimental.pallas import tpu as pltpu
from jax.sharding import PartitionSpec as P

CAP = 48
BF = jnp.bfloat16
F32 = jnp.float32


def slot_places(expert_ids, experts):
    flat_ids = expert_ids.reshape(-1)
    labels = jnp.arange(experts, dtype=jnp.int32)
    onehot = (flat_ids[:, None] == labels[None, :]).astype(jnp.int32)
    before = jnp.cumsum(onehot, axis=0, dtype=jnp.int32) - onehot
    return (jnp.sum(before * onehot, axis=1, dtype=jnp.int32), flat_ids)


def general(
    tokens,
    expert_ids,
    route_gates,
    shared_gate_vec,
    w_shared_gate,
    w_shared_up,
    w_shared_down_t,
    w_expert_gate_t,
    w_expert_up_t,
    w_expert_down,
):
    n_dp = lax.axis_size("dp")
    row_count, model_width = tokens.shape
    top_k = expert_ids.shape[1]
    exp_dev = w_expert_gate_t.shape[0]
    experts = exp_dev * n_dp
    portion_gate = lax.all_gather(w_shared_gate, "dp", axis=0, tiled=True)
    portion_up = lax.all_gather(w_shared_up, "dp", axis=0, tiled=True)
    portion_down = lax.all_gather(w_shared_down_t, "dp", axis=0, tiled=True)
    acc_gate = jnp.dot(tokens, portion_gate, preferred_element_type=jnp.float32)
    acc_up = jnp.dot(tokens, portion_up, preferred_element_type=jnp.float32)
    shared_hidden = (jax.nn.silu(acc_gate) * acc_up).astype(jnp.bfloat16)
    shared_part = lax.dot_general(
        shared_hidden, portion_down, (((1,), (1,)), ((), ())), preferred_element_type=jnp.float32
    )
    shared_scale = jax.nn.sigmoid(
        jnp.dot(tokens, shared_gate_vec, preferred_element_type=jnp.float32)
    )
    places, flat_ids = slot_places(expert_ids, experts)
    target = flat_ids * CAP + places
    source_rows = jnp.arange(row_count * top_k, dtype=jnp.int32) // top_k
    outgoing = (
        jnp.zeros((experts * CAP, model_width), jnp.bfloat16).at[target].set(tokens[source_rows])
    )
    arrived = lax.all_to_all(
        outgoing.reshape(n_dp, exp_dev * CAP, model_width),
        "dp",
        split_axis=0,
        concat_axis=0,
        tiled=True,
    )
    arrived = arrived.reshape(n_dp, exp_dev, CAP, model_width)
    ex_gate = jnp.einsum(
        "sjcd,jfd->sjcf", arrived, w_expert_gate_t, preferred_element_type=jnp.float32
    )
    ex_up = jnp.einsum("sjcd,jfd->sjcf", arrived, w_expert_up_t, preferred_element_type=jnp.float32)
    ex_hidden = (jax.nn.silu(ex_gate) * ex_up).astype(jnp.bfloat16)
    ex_part = jnp.einsum(
        "sjcf,jfd->sjcd", ex_hidden, w_expert_down, preferred_element_type=jnp.float32
    )
    returned = lax.all_to_all(
        ex_part.reshape(n_dp, exp_dev * CAP, model_width),
        "dp",
        split_axis=0,
        concat_axis=0,
        tiled=True,
    )
    returned = returned.reshape(experts * CAP, model_width)
    picked = returned[target].reshape(row_count, top_k, model_width)
    routed = jnp.sum(picked * route_gates[:, :, None], axis=1)
    combined = shared_scale[:, None] * shared_part + routed
    return lax.psum_scatter(combined, "tensor", scatter_dimension=1, tiled=True).astype(
        jnp.bfloat16
    )


def swap(x, axis, bit):
    n = lax.axis_size(axis)
    return lax.ppermute(x, axis, [(i, i ^ bit) for i in range(n)])


def vmem_full(a):
    return pl.BlockSpec(a.shape, lambda *_: (0,) * a.ndim)


ANY = pl.BlockSpec(memory_space=pl.ANY)
FULL = 60 << 20
SMEM = pl.BlockSpec(memory_space=pltpu.SMEM)


def run_all(copies):
    for c in copies:
        c.start()
    for c in copies:
        c.wait()


def token_rows(where, tokens, ids_t, gates_t):
    rows, d = tokens.shape
    top = ids_t.shape[0]
    quarter = rows // 4

    def kernel(where_ref, tok_ref, ids_ref, gates_ref, mine, tags, sem):
        at = pl.multiple_of(where_ref[1] * quarter, quarter)
        copy = pltpu.make_async_copy(
            tok_ref.at[pl.ds(at, quarter)], mine.at[:, pl.ds(0, d)], sem
        )
        copy.start()
        gates = gates_ref[...]
        high = gates.astype(BF).astype(F32)
        lines = [ids_ref[...].astype(F32), high, gates - high]
        lines.append(jnp.zeros((128 - 3 * top, rows), F32))
        tags[...] = jnp.concatenate(lines, axis=0).T
        mine[:, pl.ds(d, 128)] = tags[pl.ds(at, quarter), :].astype(BF)
        copy.wait()

    vm = pl.BlockSpec(memory_space=pltpu.VMEM)
    return pl.pallas_call(
        kernel,
        out_shape=jax.ShapeDtypeStruct((quarter, d + 128), BF),
        in_specs=[SMEM, ANY, vm, vm],
        out_specs=vm,
        scratch_shapes=[pltpu.VMEM((rows, 128), F32), pltpu.SemaphoreType.DMA],
        compiler_params=pltpu.CompilerParams(vmem_limit_bytes=FULL),
        name="token_rows",
    )(where, tokens, ids_t, gates_t)


def pack(where, wg, wu, wd, width):
    d_part, ff = wg.shape
    n = ff // (2 * width)
    whole = width - 64
    half = d_part // 2

    def kernel(where_ref, g_ref, u_ref, d_ref, *rest):
        outs_gu, outs_d = rest[:n], rest[n : 2 * n]
        gu_buf, d_buf, gu_mid, d_mid, in_sem, out_sem = rest[2 * n :]
        z, t, g = where_ref[0], where_ref[1], where_ref[2]
        side = g * (width + 64)
        loads = []
        for k in range(n):
            start = (z ^ k) * (2 * width)
            wide = pl.multiple_of(start + side, 128)
            mid = pl.multiple_of(start + whole, 128)
            jobs = []
            for m, ref in enumerate((g_ref, u_ref)):
                lane = 0 if m == 0 else width + 64
                jobs.append((ref.at[:, pl.ds(wide, whole)], gu_buf.at[k, :, pl.ds(lane, whole)]))
                jobs.append((ref.at[:, pl.ds(mid, 128)], gu_mid.at[k, m]))
            loads.append(jobs)
        for r in range(n):
            start = (t ^ r) * (2 * width)
            wide = pl.multiple_of(start + side, 128)
            mid = pl.multiple_of(start + whole, 128)
            jobs = []
            for m in range(2):
                lane = 0 if m == 0 else width + 64
                part = d_ref.at[pl.ds(m * half, half)]
                jobs.append((part.at[:, pl.ds(wide, whole)], d_buf.at[r, :, pl.ds(lane, whole)]))
                jobs.append((part.at[:, pl.ds(mid, 128)], d_mid.at[r, m]))
            loads.append(jobs)
        order = [1, 2, 3, 0, n, n + 1, n + 2, n + 3]
        copies = {}
        for i in order:
            copies[i] = [
                pltpu.make_async_copy(s, d, in_sem.at[i, j]) for j, (s, d) in enumerate(loads[i])
            ]
            for c in copies[i]:
                c.start()
        stores = []
        for i in order:
            for c in copies[i]:
                c.wait()
            buf, mids, out = (gu_buf, gu_mid, outs_gu[i]) if i < n else (d_buf, d_mid, outs_d[i - n])
            p = i % n
            first = pltpu.roll(mids[p, 0].astype(F32), 64 * g, 1)
            second = pltpu.roll(mids[p, 1].astype(F32), 64 * (1 - g), 1)
            lane = lax.broadcasted_iota(jnp.int32, first.shape, 1)
            buf[p, :, pl.ds(whole, 128)] = jnp.where(lane < 64, first, second).astype(BF)
            stores.append(pltpu.make_async_copy(buf.at[p], out, out_sem.at[i]))
            stores[-1].start()
        for c in stores:
            c.wait()

    return pl.pallas_call(
        kernel,
        out_shape=[jax.ShapeDtypeStruct((d_part, 2 * width), BF)] * n
        + [jax.ShapeDtypeStruct((half, 2 * width), BF)] * n,
        in_specs=[SMEM, ANY, ANY, ANY],
        out_specs=[ANY] * (2 * n),
        scratch_shapes=[
            pltpu.VMEM((n, d_part, 2 * width), BF),
            pltpu.VMEM((n, half, 2 * width), BF),
            pltpu.VMEM((n, 2, d_part, 128), BF),
            pltpu.VMEM((n, 2, half, 128), BF),
            pltpu.SemaphoreType.DMA((2 * n, 4)),
            pltpu.SemaphoreType.DMA((2 * n,)),
        ],
        compiler_params=pltpu.CompilerParams(vmem_limit_bytes=FULL),
        cost_estimate=pl.CostEstimate(flops=0, bytes_accessed=8 << 20, transcendentals=0),
        name="pack",
    )(where, wg, wu, wd)


def token_copies(where_ref, refs, rows_ref, info_ref, sem, base):
    t = where_ref[1]
    n_dp, quarter, _ = refs[0].shape
    d = rows_ref.shape[1]
    copies = []
    for k in range(n_dp):
        jobs = []
        for b, ref in enumerate(refs):
            row = pl.multiple_of(base + k * 4 * quarter + (t ^ b) * quarter, quarter)
            src = ref.at[k]
            jobs.append((src.at[:, pl.ds(0, d)], rows_ref.at[pl.ds(row, quarter)]))
            if info_ref is not None:
                jobs.append((src.at[:, pl.ds(d, 128)], info_ref.at[pl.ds(row, quarter)]))
        copies.append(
            [pltpu.make_async_copy(x, y, sem.at[k, j]) for j, (x, y) in enumerate(jobs)]
        )
    return copies


def routed_experts(where, spread_tokens, eg, eu, ed, top):
    e_dev, ff_e, d = eg.shape
    n_dp, quarter, _ = spread_tokens[0].shape
    block = 4 * quarter
    n_tok = n_dp * block
    part = d // 4
    pairs = n_dp // 2
    seg = 2 * CAP
    side = e_dev * seg

    def kernel(where_ref, *rest):
        refs = rest[:4]
        g_ref, u_ref, w_ref, give, keep, tok, info, back, moved, gate_of, acc_t, sem = rest[4:]
        e = pl.program_id(0)
        z, t = where_ref[0], where_ref[1]

        @pl.when(e == 0)
        def _():
            run_all(sum(token_copies(where_ref, refs, tok, info, sem, 0), []))
            tags = info[...].astype(F32)
            lane = lax.broadcasted_iota(jnp.int32, tags.shape, 1)
            weight = pltpu.roll(tags, 128 - top, 1) + pltpu.roll(tags, 128 - 2 * top, 1)
            chosen = jnp.zeros(tags.shape, F32)
            gates = jnp.zeros(tags.shape, F32)
            for i in range(e_dev):
                hit = (tags == (z * e_dev + i).astype(F32)) & (lane < top)
                has = jnp.sum(jnp.where(hit, 1.0, 0.0), axis=1, keepdims=True)
                gate = jnp.sum(jnp.where(hit, weight, 0.0), axis=1, keepdims=True)
                chosen = jnp.where(lane == i, has, chosen)
                gates = jnp.where(lane == i, gate, gates)
            row = lax.broadcasted_iota(jnp.int32, (block, block), 0)
            col = lax.broadcasted_iota(jnp.int32, (block, block), 1)
            earlier = jnp.where(col < row, 1.0, 0.0).astype(BF)
            for p in range(pairs):
                slots = []
                for b in range(2):
                    lo = (2 * p + b) * block
                    mine = chosen[lo : lo + block]
                    before = jnp.dot(earlier, mine.astype(BF), preferred_element_type=F32)
                    slots.append(jnp.where(mine > 0.5, before + b * CAP, -1.0))
                slot_t = jnp.concatenate(slots, axis=0).T
                gate_t = gates[2 * p * block : 2 * (p + 1) * block].T
                picks = []
                for i in range(e_dev):
                    spot = lax.broadcasted_iota(jnp.int32, (seg, 2 * block), 0).astype(F32)
                    hit = spot == slot_t[i : i + 1, :]
                    g = jnp.sum(jnp.where(hit, gate_t[i : i + 1, :], 0.0), axis=1, keepdims=True)
                    gate_of[pl.ds(p * side + i * seg, seg), :] = jnp.broadcast_to(g, (seg, 128))
                    picks.append(jnp.where(hit, 1.0, 0.0))
                pick = jnp.concatenate(picks, axis=0)
                back[p] = pick.T.astype(BF)
                moved[pl.ds(p * side, side), :] = jnp.dot(
                    pick.astype(BF),
                    tok[pl.ds(2 * p * block, 2 * block), :],
                    preferred_element_type=F32,
                ).astype(BF)

        spots = [pl.ds(pl.multiple_of(p * side + e * seg, seg), seg) for p in range(pairs)]
        x = jnp.concatenate([moved[s, :] for s in spots], axis=0)
        dims = (((1,), (1,)), ((), ()))
        gate = lax.dot_general(x, g_ref[0], dims, preferred_element_type=F32)
        up = lax.dot_general(x, u_ref[0], dims, preferred_element_type=F32)
        hidden = (gate * jax.nn.sigmoid(gate) * up).astype(BF)
        out = jnp.dot(hidden, w_ref[0], preferred_element_type=F32)
        for p, s in enumerate(spots):
            moved[s, :] = (gate_of[s, :1] * out[p * seg : (p + 1) * seg]).astype(BF)

        @pl.when(e == e_dev - 1)
        def _():
            for p in range(pairs):
                for i in range(d // 256):
                    sums = jnp.dot(
                        back[p],
                        moved[pl.ds(p * side, side), pl.ds(256 * i, 256)],
                        preferred_element_type=F32,
                    )
                    acc_t[pl.ds(256 * i, 256), pl.ds(2 * p * block, 2 * block)] = sums.T
            for b in range(2):
                mine = pl.multiple_of((t ^ (2 * b)) * part, part)
                theirs = pl.multiple_of((t ^ (2 * b + 1)) * part, part)
                keep[b] = acc_t[pl.ds(mine, part), :]
                give[b] = acc_t[pl.ds(theirs, part), :].astype(BF)

    weights = pl.BlockSpec((1, ff_e, d), lambda e: (e, 0, 0))
    return pl.pallas_call(
        kernel,
        grid=(e_dev,),
        out_shape=[
            jax.ShapeDtypeStruct((2, part, n_tok), BF),
            jax.ShapeDtypeStruct((2, part, n_tok), F32),
        ],
        in_specs=[SMEM] + [ANY] * 4 + [weights, weights, weights],
        out_specs=[
            pl.BlockSpec((2, part, n_tok), lambda e: (0, 0, 0)),
            pl.BlockSpec((2, part, n_tok), lambda e: (0, 0, 0)),
        ],
        scratch_shapes=[
            pltpu.VMEM((n_tok, d), BF),
            pltpu.VMEM((n_tok, 128), BF),
            pltpu.VMEM((pairs, 2 * block, side), BF),
            pltpu.VMEM((pairs * side, d), BF),
            pltpu.VMEM((pairs * side, 128), F32),
            pltpu.VMEM((d, n_tok), F32),
            pltpu.SemaphoreType.DMA((n_dp, 8)),
        ],
        compiler_params=pltpu.CompilerParams(vmem_limit_bytes=52 << 20),
        cost_estimate=pl.CostEstimate(
            flops=6 * pairs * side * ff_e * d,
            bytes_accessed=6 * e_dev * ff_e * d,
            transcendentals=pairs * side * ff_e,
        ),
        name="routed",
    )(where, *spread_tokens, eg, eu, ed)


def shared_hidden(where, tokens, pieces, vec, after, width):
    d_part = pieces[0].shape[0]
    n = len(pieces)
    d = n * d_part
    n_dp, quarter, _ = tokens[0].shape
    n_tok = n_dp * quarter * 4
    half = n_tok // 2
    whole = width - 64

    def kernel(where_ref, *rest):
        refs, vec_ref, p_refs = rest[:4], rest[4], rest[5 : 5 + n]
        hid, scale, tok, w, tok_sem, w_sem = rest[6 + n :]
        z = where_ref[0]
        w_copies = []
        for k in range(n):
            row = pl.multiple_of((z ^ k) * d_part, d_part)
            w_copies.append(
                pltpu.make_async_copy(p_refs[k], w.at[pl.ds(row, d_part)], w_sem.at[k])
            )
        copies = token_copies(where_ref, refs, tok, None, tok_sem, 0)
        for batch in [w_copies] + copies:
            for c in batch:
                c.start()
        dims = (((1,), (1,)), ((), ()))
        lines = jnp.broadcast_to(vec_ref[...], (8, d))
        for c in w_copies:
            c.wait()
        mids = []
        for side in range(2):
            for k in range(side * n_dp // 2, (side + 1) * n_dp // 2):
                for c in copies[k]:
                    c.wait()
            rows = pl.ds(side * half, half)
            x = tok[rows, :]
            acc = jnp.dot(x, w[...], preferred_element_type=F32)
            gate_mid = acc[:, whole : whole + 128]
            up_mid = pltpu.roll(gate_mid, 64, 1)
            gate, up = acc[:, :whole], acc[:, width + 64 :]
            line = lax.dot_general(lines, x, dims, preferred_element_type=F32)
            scale[:, rows] = jax.nn.sigmoid(line[:1])
            at = pl.ds(side * (width + 64), whole)
            hid[:, at] = (gate * jax.nn.sigmoid(gate) * up).astype(BF)
            mids.append(gate_mid * jax.nn.sigmoid(gate_mid) * up_mid)
        lane = lax.broadcasted_iota(jnp.int32, mids[0].shape, 1)
        mid = jnp.where(lane < 64, mids[0], pltpu.roll(mids[1], 64, 1))
        hid[:, pl.ds(whole, 128)] = mid.astype(BF)

    vm = pl.BlockSpec(memory_space=pltpu.VMEM)
    return pl.pallas_call(
        kernel,
        out_shape=[
            jax.ShapeDtypeStruct((half, 2 * width), BF),
            jax.ShapeDtypeStruct((1, n_tok), F32),
        ],
        in_specs=[SMEM] + [ANY] * 4 + [vm] + [ANY] * (n + 1),
        out_specs=[vm] * 2,
        scratch_shapes=[
            pltpu.VMEM((n_tok, d), BF),
            pltpu.VMEM((d, 2 * width), BF),
            pltpu.SemaphoreType.DMA((n_dp, 4)),
            pltpu.SemaphoreType.DMA((n,)),
        ],
        compiler_params=pltpu.CompilerParams(vmem_limit_bytes=24 << 20),
        cost_estimate=pl.CostEstimate(
            flops=2 * n_tok * d * 2 * width,
            bytes_accessed=4 << 20,
            transcendentals=n_tok * width,
        ),
        name="shared_hidden",
    )(where, *tokens, vec, *pieces, after)


def shared_down(where, pieces, hidden, scale, width, far, routed):
    n = len(pieces)
    half = pieces[0].shape[0]
    whole = width - 64
    lanes = whole + 128
    rows_h = hidden[0].shape[0]
    n_tok = 2 * rows_h

    def kernel(where_ref, scale_ref, *rest):
        h_refs, p_refs = rest[:4], rest[4 : 4 + n]
        if far:
            out_ref, w, h, w_sem, h_sem = rest[4 + n :]
        else:
            routed_ref, out_ref, w, h, w_sem, h_sem = rest[4 + n :]
        z, t = where_ref[0], where_ref[1]
        copies = []
        for r in range(n):
            jobs = (
                (p_refs[r].at[:, pl.ds(0, lanes)], w.at[pl.ds(0, half), pl.ds(lanes * r, lanes)]),
                (
                    p_refs[r].at[:, pl.ds(lanes, whole)],
                    w.at[pl.ds(half, half), pl.ds(lanes * r, whole)],
                ),
                (
                    p_refs[r].at[:, pl.ds(whole, 128)],
                    w.at[pl.ds(half, half), pl.ds(lanes * r + whole, 128)],
                ),
            )
            for j, (s, d) in enumerate(jobs):
                copies.append(pltpu.make_async_copy(s, d, w_sem.at[r, j]))
        for m in range(4):
            at = pl.multiple_of((z ^ t ^ m) * lanes, lanes)
            top, bottom = h.at[pl.ds(0, rows_h)], h.at[pl.ds(rows_h, rows_h)]
            jobs = (
                (h_refs[m].at[:, pl.ds(0, lanes)], top.at[:, pl.ds(at, lanes)]),
                (h_refs[m].at[:, pl.ds(lanes, whole)], bottom.at[:, pl.ds(at, whole)]),
                (h_refs[m].at[:, pl.ds(whole, 128)], bottom.at[:, pl.ds(at + whole, 128)]),
            )
            for j, (s, d) in enumerate(jobs):
                copies.append(pltpu.make_async_copy(s, d, h_sem.at[m, j]))
        run_all(copies)
        low = lax.broadcasted_iota(jnp.int32, (half, 128), 1) < 64
        low_h = lax.broadcasted_iota(jnp.int32, (rows_h, 128), 1) < 64
        for r in range(n):
            at = pl.ds(lanes * r + whole, 128)
            for i in range(2):
                rows = pl.ds(half * i, half)
                mask = low if i == 0 else ~low
                w[rows, at] = jnp.where(mask, w[rows, at].astype(F32), 0.0).astype(BF)
            for i in range(2):
                rows = pl.ds(rows_h * i, rows_h)
                mid = h[rows, at].astype(F32)
                mask = low_h if i == 0 else ~low_h
                h[rows, at] = jnp.where(mask, mid, pltpu.roll(mid, 64, 1)).astype(BF)
        dims = (((1,), (1,)), ((), ()))
        out = lax.dot_general(w[...], h[...], dims, preferred_element_type=F32)
        if far:
            out_ref[...] = (out * scale_ref[...]).astype(BF)
        else:
            out_ref[...] = out * scale_ref[...] + routed_ref[...]

    vm = pl.BlockSpec(memory_space=pltpu.VMEM)
    return pl.pallas_call(
        kernel,
        out_shape=jax.ShapeDtypeStruct((2 * half, n_tok), BF if far else F32),
        in_specs=[SMEM, vm] + [ANY] * (4 + n) + ([] if far else [vm]),
        out_specs=vm,
        scratch_shapes=[
            pltpu.VMEM((2 * half, n * lanes), BF),
            pltpu.VMEM((n_tok, n * lanes), BF),
            pltpu.SemaphoreType.DMA((n, 3)),
            pltpu.SemaphoreType.DMA((4, 3)),
        ],
        compiler_params=pltpu.CompilerParams(vmem_limit_bytes=24 << 20),
        cost_estimate=pl.CostEstimate(
            flops=2 * 2 * half * n * lanes * n_tok, bytes_accessed=4 << 20, transcendentals=0
        ),
        name="down_far" if far else "down_near",
    )(where, scale, *hidden, *pieces, *([] if far else [routed]))


def exchanged(
    tokens,
    expert_ids,
    route_gates,
    shared_gate_vec,
    w_shared_gate,
    w_shared_up,
    w_shared_down_t,
    w_expert_gate_t,
    w_expert_up_t,
    w_expert_down,
):
    z, t, g = lax.axis_index("dp"), lax.axis_index("tensor"), lax.axis_index("groups")
    n_dp, n_t, n_g = lax.axis_size("dp"), lax.axis_size("tensor"), lax.axis_size("groups")
    where = jnp.stack([z, t, g]).astype(jnp.int32)
    rows, d = tokens.shape
    top = expert_ids.shape[1]
    width = w_shared_gate.shape[1] // (n_dp * n_g)

    some = where[0] >= 0

    def apart(step, *operands):
        shapes = jax.eval_shape(step, *operands)
        empty = lambda *_: jax.tree.map(lambda a: jnp.zeros(a.shape, a.dtype), shapes)
        return lax.cond(some, step, empty, *operands)

    def first_step(mine, *weights):
        packed = pack(where, *weights, width)
        over_z = jnp.stack([mine] + [swap(mine, "dp", k) for k in range(1, n_dp)])
        return over_z, packed

    over_z, packed = apart(
        first_step,
        token_rows(where, tokens, expert_ids.T, route_gates.T),
        w_shared_gate,
        w_shared_up,
        w_shared_down_t,
    )
    gu = [packed[0]] + [swap(packed[k], "dp", k) for k in range(1, n_dp)]

    def cross(piece, r):
        route = [(i * n_t + j, (j ^ r) * n_t + i) for i in range(n_dp) for j in range(n_t)]
        return lax.ppermute(piece, ("dp", "tensor"), route)

    def routed_step(q, *weights):
        over_x, other = swap(q, "tensor", 2), swap(q, "groups", 1)
        over_core = swap(q, "tensor", 1)
        over_x, other = lax.optimization_barrier((over_x, other))
        over_both, other = lax.optimization_barrier((swap(over_x, "tensor", 1), other))
        other_x = swap(other, "tensor", 2)
        own = (q, over_core, over_x, over_both)
        give, keep = routed_experts(where, own, *weights, top)
        other, other_x, give = lax.optimization_barrier((other, other_x, give))
        others = (other, swap(other, "tensor", 1), other_x, swap(other_x, "tensor", 1))
        others, give = lax.optimization_barrier((others, give))
        return own, others, swap(give, "tensor", 1), keep

    tok_own, tok_other, got, keep = apart(
        routed_step, over_z, w_expert_gate_t, w_expert_up_t, w_expert_down
    )
    vec = shared_gate_vec[None, :]
    far_hidden, far_scale = shared_hidden(where, tok_other, gu, vec, got, width)

    def gather_step(h, tokens_here, pieces):
        over_x = swap(h, "tensor", 2)
        near = shared_hidden(where, tokens_here, pieces, vec, h, width)
        over_x, near = lax.optimization_barrier((over_x, near))
        return [h, swap(h, "tensor", 1), over_x, swap(over_x, "tensor", 1)], near

    far_hidden, first = lax.optimization_barrier((far_hidden, cross(packed[n_dp], 0)))
    gathered, (near_hidden, near_scale) = apart(gather_step, far_hidden, tok_own, gu)
    near_x, near_core = swap(near_hidden, "tensor", 2), swap(near_hidden, "tensor", 1)
    down = [first] + [cross(packed[n_dp + r], r) for r in range(1, n_dp)]
    far = shared_down(where, down, gathered, far_scale, width, True, None)
    got = got.astype(F32)
    routed = keep[0] + got[0]
    routed_far = (keep[1] + got[1]).astype(BF)
    gathered = [near_hidden, near_core, near_x, swap(near_x, "tensor", 1)]
    near = shared_down(where, down, gathered, near_scale, width, False, routed)
    total = near + swap(far, "groups", 1).astype(F32) + swap(routed_far, "tensor", 2).astype(F32)
    done = total[:, :rows]
    for k in range(1, n_dp):
        piece = total[:, rows * k : rows * (k + 1)].astype(BF)
        done = done + swap(piece, "dp", k).astype(F32)
    return done.T.astype(BF)


def solution(mesh):
    sizes = mesh.shape

    def on_device(*args):
        d_part, ff = args[4].shape
        width = ff // (sizes["dp"] * sizes["groups"])
        fits = (
            sizes["dp"] == 4
            and sizes["tensor"] == 4
            and sizes["groups"] == 2
            and width % 128 == 64
            and d_part % 32 == 0
            and args[7].shape[2] % 256 == 0
            and args[1].shape[1] == 8
            and args[0].shape[0] % 128 == 0
        )
        return (exchanged if fits else general)(*args)

    return jax.shard_map(
        on_device,
        mesh=mesh,
        in_specs=(
            P(("groups", "dp"), None),
            P(("groups", "dp"), None),
            P(("groups", "dp"), None),
            P(),
            P("dp", "tensor"),
            P("dp", "tensor"),
            P("dp", "tensor"),
            P("dp", "tensor", None),
            P("dp", "tensor", None),
            P("dp", "tensor", None),
        ),
        out_specs=P(("groups", "dp"), "tensor"),
        check_vma=False,
    )
```

```python
import jax
import jax.numpy as jnp
from jax import lax
from jax.experimental import pallas as pl
from jax.experimental.pallas import tpu as pltpu
from jax.sharding import PartitionSpec as P

CAP = 48
BF = jnp.bfloat16
F32 = jnp.float32


def slot_places(expert_ids, experts):
    flat_ids = expert_ids.reshape(-1)
    labels = jnp.arange(experts, dtype=jnp.int32)
    onehot = (flat_ids[:, None] == labels[None, :]).astype(jnp.int32)
    before = jnp.cumsum(onehot, axis=0, dtype=jnp.int32) - onehot
    return (jnp.sum(before * onehot, axis=1, dtype=jnp.int32), flat_ids)


def general(
    tokens,
    expert_ids,
    route_gates,
    shared_gate_vec,
    w_shared_gate,
    w_shared_up,
    w_shared_down_t,
    w_expert_gate_t,
    w_expert_up_t,
    w_expert_down,
):
    n_dp = lax.axis_size("dp")
    row_count, model_width = tokens.shape
    top_k = expert_ids.shape[1]
    exp_dev = w_expert_gate_t.shape[0]
    experts = exp_dev * n_dp
    portion_gate = lax.all_gather(w_shared_gate, "dp", axis=0, tiled=True)
    portion_up = lax.all_gather(w_shared_up, "dp", axis=0, tiled=True)
    portion_down = lax.all_gather(w_shared_down_t, "dp", axis=0, tiled=True)
    acc_gate = jnp.dot(tokens, portion_gate, preferred_element_type=jnp.float32)
    acc_up = jnp.dot(tokens, portion_up, preferred_element_type=jnp.float32)
    shared_hidden = (jax.nn.silu(acc_gate) * acc_up).astype(jnp.bfloat16)
    shared_part = lax.dot_general(
        shared_hidden, portion_down, (((1,), (1,)), ((), ())), preferred_element_type=jnp.float32
    )
    shared_scale = jax.nn.sigmoid(
        jnp.dot(tokens, shared_gate_vec, preferred_element_type=jnp.float32)
    )
    places, flat_ids = slot_places(expert_ids, experts)
    target = flat_ids * CAP + places
    source_rows = jnp.arange(row_count * top_k, dtype=jnp.int32) // top_k
    outgoing = (
        jnp.zeros((experts * CAP, model_width), jnp.bfloat16).at[target].set(tokens[source_rows])
    )
    arrived = lax.all_to_all(
        outgoing.reshape(n_dp, exp_dev * CAP, model_width),
        "dp",
        split_axis=0,
        concat_axis=0,
        tiled=True,
    )
    arrived = arrived.reshape(n_dp, exp_dev, CAP, model_width)
    ex_gate = jnp.einsum(
        "sjcd,jfd->sjcf", arrived, w_expert_gate_t, preferred_element_type=jnp.float32
    )
    ex_up = jnp.einsum("sjcd,jfd->sjcf", arrived, w_expert_up_t, preferred_element_type=jnp.float32)
    ex_hidden = (jax.nn.silu(ex_gate) * ex_up).astype(jnp.bfloat16)
    ex_part = jnp.einsum(
        "sjcf,jfd->sjcd", ex_hidden, w_expert_down, preferred_element_type=jnp.float32
    )
    returned = lax.all_to_all(
        ex_part.reshape(n_dp, exp_dev * CAP, model_width),
        "dp",
        split_axis=0,
        concat_axis=0,
        tiled=True,
    )
    returned = returned.reshape(experts * CAP, model_width)
    picked = returned[target].reshape(row_count, top_k, model_width)
    routed = jnp.sum(picked * route_gates[:, :, None], axis=1)
    combined = shared_scale[:, None] * shared_part + routed
    return lax.psum_scatter(combined, "tensor", scatter_dimension=1, tiled=True).astype(
        jnp.bfloat16
    )


def swap(x, axis, bit):
    n = lax.axis_size(axis)
    return lax.ppermute(x, axis, [(i, i ^ bit) for i in range(n)])


def vmem_full(a):
    return pl.BlockSpec(a.shape, lambda *_: (0,) * a.ndim)


ANY = pl.BlockSpec(memory_space=pl.ANY)
FULL = 60 << 20
SMEM = pl.BlockSpec(memory_space=pltpu.SMEM)


def run_all(copies):
    for c in copies:
        c.start()
    for c in copies:
        c.wait()


def token_rows(where, tokens, ids_t, gates_t):
    rows, d = tokens.shape
    top = ids_t.shape[0]
    quarter = rows // 4

    def kernel(where_ref, tok_ref, ids_ref, gates_ref, mine, tags, sem):
        at = pl.multiple_of(where_ref[1] * quarter, quarter)
        copy = pltpu.make_async_copy(
            tok_ref.at[pl.ds(at, quarter)], mine.at[:, pl.ds(0, d)], sem
        )
        copy.start()
        gates = gates_ref[...]
        high = gates.astype(BF).astype(F32)
        lines = [ids_ref[...].astype(F32), high, gates - high]
        lines.append(jnp.zeros((128 - 3 * top, rows), F32))
        tags[...] = jnp.concatenate(lines, axis=0).T
        mine[:, pl.ds(d, 128)] = tags[pl.ds(at, quarter), :].astype(BF)
        copy.wait()

    vm = pl.BlockSpec(memory_space=pltpu.VMEM)
    return pl.pallas_call(
        kernel,
        out_shape=jax.ShapeDtypeStruct((quarter, d + 128), BF),
        in_specs=[SMEM, ANY, vm, vm],
        out_specs=vm,
        scratch_shapes=[pltpu.VMEM((rows, 128), F32), pltpu.SemaphoreType.DMA],
        compiler_params=pltpu.CompilerParams(vmem_limit_bytes=FULL),
        name="token_rows",
    )(where, tokens, ids_t, gates_t)


def pack(where, wg, wu, wd, width):
    d_part, ff = wg.shape
    n = ff // (2 * width)
    whole = width - 64
    half = d_part // 2

    def kernel(where_ref, g_ref, u_ref, d_ref, *rest):
        outs_gu, outs_d = rest[:n], rest[n : 2 * n]
        gu_buf, d_buf, gu_mid, d_mid, in_sem, out_sem = rest[2 * n :]
        z, t, g = where_ref[0], where_ref[1], where_ref[2]
        side = g * (width + 64)
        loads = []
        for k in range(n):
            start = (z ^ k) * (2 * width)
            wide = pl.multiple_of(start + side, 128)
            mid = pl.multiple_of(start + whole, 128)
            jobs = []
            for m, ref in enumerate((g_ref, u_ref)):
                lane = 0 if m == 0 else width + 64
                jobs.append((ref.at[:, pl.ds(wide, whole)], gu_buf.at[k, :, pl.ds(lane, whole)]))
                jobs.append((ref.at[:, pl.ds(mid, 128)], gu_mid.at[k, m]))
            loads.append(jobs)
        for r in range(n):
            start = (t ^ r) * (2 * width)
            wide = pl.multiple_of(start + side, 128)
            mid = pl.multiple_of(start + whole, 128)
            jobs = []
            for m in range(2):
                lane = 0 if m == 0 else width + 64
                part = d_ref.at[pl.ds(m * half, half)]
                jobs.append((part.at[:, pl.ds(wide, whole)], d_buf.at[r, :, pl.ds(lane, whole)]))
                jobs.append((part.at[:, pl.ds(mid, 128)], d_mid.at[r, m]))
            loads.append(jobs)
        order = [1, 2, 3, 0, n, n + 1, n + 2, n + 3]
        copies = {}
        for i in order:
            copies[i] = [
                pltpu.make_async_copy(s, d, in_sem.at[i, j]) for j, (s, d) in enumerate(loads[i])
            ]
            for c in copies[i]:
                c.start()
        stores = []
        for i in order:
            for c in copies[i]:
                c.wait()
            buf, mids, out = (gu_buf, gu_mid, outs_gu[i]) if i < n else (d_buf, d_mid, outs_d[i - n])
            p = i % n
            first = pltpu.roll(mids[p, 0].astype(F32), 64 * g, 1)
            second = pltpu.roll(mids[p, 1].astype(F32), 64 * (1 - g), 1)
            lane = lax.broadcasted_iota(jnp.int32, first.shape, 1)
            buf[p, :, pl.ds(whole, 128)] = jnp.where(lane < 64, first, second).astype(BF)
            stores.append(pltpu.make_async_copy(buf.at[p], out, out_sem.at[i]))
            stores[-1].start()
        for c in stores:
            c.wait()

    return pl.pallas_call(
        kernel,
        out_shape=[jax.ShapeDtypeStruct((d_part, 2 * width), BF)] * n
        + [jax.ShapeDtypeStruct((half, 2 * width), BF)] * n,
        in_specs=[SMEM, ANY, ANY, ANY],
        out_specs=[ANY] * (2 * n),
        scratch_shapes=[
            pltpu.VMEM((n, d_part, 2 * width), BF),
            pltpu.VMEM((n, half, 2 * width), BF),
            pltpu.VMEM((n, 2, d_part, 128), BF),
            pltpu.VMEM((n, 2, half, 128), BF),
            pltpu.SemaphoreType.DMA((2 * n, 4)),
            pltpu.SemaphoreType.DMA((2 * n,)),
        ],
        compiler_params=pltpu.CompilerParams(vmem_limit_bytes=FULL),
        cost_estimate=pl.CostEstimate(flops=0, bytes_accessed=8 << 20, transcendentals=0),
        name="pack",
    )(where, wg, wu, wd)


def token_copies(where_ref, refs, rows_ref, info_ref, sem, base):
    t = where_ref[1]
    n_dp, quarter, _ = refs[0].shape
    d = rows_ref.shape[1]
    copies = []
    for k in range(n_dp):
        jobs = []
        for b, ref in enumerate(refs):
            row = pl.multiple_of(base + k * 4 * quarter + (t ^ b) * quarter, quarter)
            src = ref.at[k]
            jobs.append((src.at[:, pl.ds(0, d)], rows_ref.at[pl.ds(row, quarter)]))
            if info_ref is not None:
                jobs.append((src.at[:, pl.ds(d, 128)], info_ref.at[pl.ds(row, quarter)]))
        copies.append(
            [pltpu.make_async_copy(x, y, sem.at[k, j]) for j, (x, y) in enumerate(jobs)]
        )
    return copies


def routed_experts(where, spread_tokens, eg, eu, ed, top):
    e_dev, ff_e, d = eg.shape
    n_dp, quarter, _ = spread_tokens[0].shape
    block = 4 * quarter
    n_tok = n_dp * block
    part = d // 4
    pairs = n_dp // 2
    seg = 2 * CAP
    side = e_dev * seg

    def kernel(where_ref, *rest):
        refs = rest[:4]
        g_ref, u_ref, w_ref, give, keep, tok, info, back, moved, gate_of, acc_t, sem = rest[4:]
        e = pl.program_id(0)
        z, t = where_ref[0], where_ref[1]

        @pl.when(e == 0)
        def _():
            run_all(sum(token_copies(where_ref, refs, tok, info, sem, 0), []))
            tags = info[...].astype(F32)
            lane = lax.broadcasted_iota(jnp.int32, tags.shape, 1)
            weight = pltpu.roll(tags, 128 - top, 1) + pltpu.roll(tags, 128 - 2 * top, 1)
            chosen = jnp.zeros(tags.shape, F32)
            gates = jnp.zeros(tags.shape, F32)
            for i in range(e_dev):
                hit = (tags == (z * e_dev + i).astype(F32)) & (lane < top)
                has = jnp.sum(jnp.where(hit, 1.0, 0.0), axis=1, keepdims=True)
                gate = jnp.sum(jnp.where(hit, weight, 0.0), axis=1, keepdims=True)
                chosen = jnp.where(lane == i, has, chosen)
                gates = jnp.where(lane == i, gate, gates)
            row = lax.broadcasted_iota(jnp.int32, (block, block), 0)
            col = lax.broadcasted_iota(jnp.int32, (block, block), 1)
            earlier = jnp.where(col < row, 1.0, 0.0).astype(BF)
            for p in range(pairs):
                slots = []
                for b in range(2):
                    lo = (2 * p + b) * block
                    mine = chosen[lo : lo + block]
                    before = jnp.dot(earlier, mine.astype(BF), preferred_element_type=F32)
                    slots.append(jnp.where(mine > 0.5, before + b * CAP, -1.0))
                slot_t = jnp.concatenate(slots, axis=0).T
                gate_t = gates[2 * p * block : 2 * (p + 1) * block].T
                picks = []
                for i in range(e_dev):
                    spot = lax.broadcasted_iota(jnp.int32, (seg, 2 * block), 0).astype(F32)
                    hit = spot == slot_t[i : i + 1, :]
                    g = jnp.sum(jnp.where(hit, gate_t[i : i + 1, :], 0.0), axis=1, keepdims=True)
                    gate_of[pl.ds(p * side + i * seg, seg), :] = jnp.broadcast_to(g, (seg, 128))
                    picks.append(jnp.where(hit, 1.0, 0.0))
                pick = jnp.concatenate(picks, axis=0)
                back[p] = pick.T.astype(BF)
                moved[pl.ds(p * side, side), :] = jnp.dot(
                    pick.astype(BF),
                    tok[pl.ds(2 * p * block, 2 * block), :],
                    preferred_element_type=F32,
                ).astype(BF)

        spots = [pl.ds(pl.multiple_of(p * side + e * seg, seg), seg) for p in range(pairs)]
        x = jnp.concatenate([moved[s, :] for s in spots], axis=0)
        dims = (((1,), (1,)), ((), ()))
        gate = lax.dot_general(x, g_ref[0], dims, preferred_element_type=F32)
        up = lax.dot_general(x, u_ref[0], dims, preferred_element_type=F32)
        hidden = (gate * jax.nn.sigmoid(gate) * up).astype(BF)
        out = jnp.dot(hidden, w_ref[0], preferred_element_type=F32)
        for p, s in enumerate(spots):
            moved[s, :] = (gate_of[s, :1] * out[p * seg : (p + 1) * seg]).astype(BF)

        @pl.when(e == e_dev - 1)
        def _():
            for p in range(pairs):
                for i in range(d // 256):
                    sums = jnp.dot(
                        back[p],
                        moved[pl.ds(p * side, side), pl.ds(256 * i, 256)],
                        preferred_element_type=F32,
                    )
                    acc_t[pl.ds(256 * i, 256), pl.ds(2 * p * block, 2 * block)] = sums.T
            for b in range(2):
                mine = pl.multiple_of((t ^ (2 * b)) * part, part)
                theirs = pl.multiple_of((t ^ (2 * b + 1)) * part, part)
                keep[b] = acc_t[pl.ds(mine, part), :]
                give[b] = acc_t[pl.ds(theirs, part), :].astype(BF)

    weights = pl.BlockSpec((1, ff_e, d), lambda e: (e, 0, 0))
    return pl.pallas_call(
        kernel,
        grid=(e_dev,),
        out_shape=[
            jax.ShapeDtypeStruct((2, part, n_tok), BF),
            jax.ShapeDtypeStruct((2, part, n_tok), F32),
        ],
        in_specs=[SMEM] + [ANY] * 4 + [weights, weights, weights],
        out_specs=[
            pl.BlockSpec((2, part, n_tok), lambda e: (0, 0, 0)),
            pl.BlockSpec((2, part, n_tok), lambda e: (0, 0, 0)),
        ],
        scratch_shapes=[
            pltpu.VMEM((n_tok, d), BF),
            pltpu.VMEM((n_tok, 128), BF),
            pltpu.VMEM((pairs, 2 * block, side), BF),
            pltpu.VMEM((pairs * side, d), BF),
            pltpu.VMEM((pairs * side, 128), F32),
            pltpu.VMEM((d, n_tok), F32),
            pltpu.SemaphoreType.DMA((n_dp, 8)),
        ],
        compiler_params=pltpu.CompilerParams(vmem_limit_bytes=52 << 20),
        cost_estimate=pl.CostEstimate(
            flops=6 * pairs * side * ff_e * d,
            bytes_accessed=6 * e_dev * ff_e * d,
            transcendentals=pairs * side * ff_e,
        ),
        name="routed",
    )(where, *spread_tokens, eg, eu, ed)


def shared_hidden(where, tokens, pieces, vec, after, width):
    d_part = pieces[0].shape[0]
    n = len(pieces)
    d = n * d_part
    n_dp, quarter, _ = tokens[0].shape
    n_tok = n_dp * quarter * 4
    half = n_tok // 2
    whole = width - 64

    def kernel(where_ref, *rest):
        refs, vec_ref, p_refs = rest[:4], rest[4], rest[5 : 5 + n]
        hid, scale, tok, w, tok_sem, w_sem = rest[6 + n :]
        z = where_ref[0]
        w_copies = []
        for k in range(n):
            row = pl.multiple_of((z ^ k) * d_part, d_part)
            w_copies.append(
                pltpu.make_async_copy(p_refs[k], w.at[pl.ds(row, d_part)], w_sem.at[k])
            )
        copies = token_copies(where_ref, refs, tok, None, tok_sem, 0)
        for batch in [w_copies] + copies:
            for c in batch:
                c.start()
        dims = (((1,), (1,)), ((), ()))
        lines = jnp.broadcast_to(vec_ref[...], (8, d))
        for c in w_copies:
            c.wait()
        mids = []
        for side in range(2):
            for k in range(side * n_dp // 2, (side + 1) * n_dp // 2):
                for c in copies[k]:
                    c.wait()
            rows = pl.ds(side * half, half)
            x = tok[rows, :]
            acc = jnp.dot(x, w[...], preferred_element_type=F32)
            gate_mid = acc[:, whole : whole + 128]
            up_mid = pltpu.roll(gate_mid, 64, 1)
            gate, up = acc[:, :whole], acc[:, width + 64 :]
            line = lax.dot_general(lines, x, dims, preferred_element_type=F32)
            scale[:, rows] = jax.nn.sigmoid(line[:1])
            at = pl.ds(side * (width + 64), whole)
            hid[:, at] = (gate * jax.nn.sigmoid(gate) * up).astype(BF)
            mids.append(gate_mid * jax.nn.sigmoid(gate_mid) * up_mid)
        lane = lax.broadcasted_iota(jnp.int32, mids[0].shape, 1)
        mid = jnp.where(lane < 64, mids[0], pltpu.roll(mids[1], 64, 1))
        hid[:, pl.ds(whole, 128)] = mid.astype(BF)

    vm = pl.BlockSpec(memory_space=pltpu.VMEM)
    return pl.pallas_call(
        kernel,
        out_shape=[
            jax.ShapeDtypeStruct((half, 2 * width), BF),
            jax.ShapeDtypeStruct((1, n_tok), F32),
        ],
        in_specs=[SMEM] + [ANY] * 4 + [vm] + [ANY] * (n + 1),
        out_specs=[vm] * 2,
        scratch_shapes=[
            pltpu.VMEM((n_tok, d), BF),
            pltpu.VMEM((d, 2 * width), BF),
            pltpu.SemaphoreType.DMA((n_dp, 4)),
            pltpu.SemaphoreType.DMA((n,)),
        ],
        compiler_params=pltpu.CompilerParams(vmem_limit_bytes=24 << 20),
        cost_estimate=pl.CostEstimate(
            flops=2 * n_tok * d * 2 * width,
            bytes_accessed=4 << 20,
            transcendentals=n_tok * width,
        ),
        name="shared_hidden",
    )(where, *tokens, vec, *pieces, after)


def shared_down(where, pieces, hidden, scale, width, far, routed):
    n = len(pieces)
    half = pieces[0].shape[0]
    whole = width - 64
    lanes = whole + 128
    rows_h = hidden[0].shape[0]
    n_tok = 2 * rows_h

    def kernel(where_ref, scale_ref, *rest):
        h_refs, p_refs = rest[:4], rest[4 : 4 + n]
        if far:
            out_ref, w, h, w_sem, h_sem = rest[4 + n :]
        else:
            routed_ref, out_ref, w, h, w_sem, h_sem = rest[4 + n :]
        z, t = where_ref[0], where_ref[1]
        copies = []
        for r in range(n):
            jobs = (
                (p_refs[r].at[:, pl.ds(0, lanes)], w.at[pl.ds(0, half), pl.ds(lanes * r, lanes)]),
                (
                    p_refs[r].at[:, pl.ds(lanes, whole)],
                    w.at[pl.ds(half, half), pl.ds(lanes * r, whole)],
                ),
                (
                    p_refs[r].at[:, pl.ds(whole, 128)],
                    w.at[pl.ds(half, half), pl.ds(lanes * r + whole, 128)],
                ),
            )
            for j, (s, d) in enumerate(jobs):
                copies.append(pltpu.make_async_copy(s, d, w_sem.at[r, j]))
        for m in range(4):
            at = pl.multiple_of((z ^ t ^ m) * lanes, lanes)
            top, bottom = h.at[pl.ds(0, rows_h)], h.at[pl.ds(rows_h, rows_h)]
            jobs = (
                (h_refs[m].at[:, pl.ds(0, lanes)], top.at[:, pl.ds(at, lanes)]),
                (h_refs[m].at[:, pl.ds(lanes, whole)], bottom.at[:, pl.ds(at, whole)]),
                (h_refs[m].at[:, pl.ds(whole, 128)], bottom.at[:, pl.ds(at + whole, 128)]),
            )
            for j, (s, d) in enumerate(jobs):
                copies.append(pltpu.make_async_copy(s, d, h_sem.at[m, j]))
        run_all(copies)
        low = lax.broadcasted_iota(jnp.int32, (half, 128), 1) < 64
        low_h = lax.broadcasted_iota(jnp.int32, (rows_h, 128), 1) < 64
        for r in range(n):
            at = pl.ds(lanes * r + whole, 128)
            for i in range(2):
                rows = pl.ds(half * i, half)
                mask = low if i == 0 else ~low
                w[rows, at] = jnp.where(mask, w[rows, at].astype(F32), 0.0).astype(BF)
            for i in range(2):
                rows = pl.ds(rows_h * i, rows_h)
                mid = h[rows, at].astype(F32)
                mask = low_h if i == 0 else ~low_h
                h[rows, at] = jnp.where(mask, mid, pltpu.roll(mid, 64, 1)).astype(BF)
        dims = (((1,), (1,)), ((), ()))
        out = lax.dot_general(w[...], h[...], dims, preferred_element_type=F32)
        if far:
            out_ref[...] = (out * scale_ref[...]).astype(BF)
        else:
            out_ref[...] = out * scale_ref[...] + routed_ref[...]

    vm = pl.BlockSpec(memory_space=pltpu.VMEM)
    return pl.pallas_call(
        kernel,
        out_shape=jax.ShapeDtypeStruct((2 * half, n_tok), BF if far else F32),
        in_specs=[SMEM, vm] + [ANY] * (4 + n) + ([] if far else [vm]),
        out_specs=vm,
        scratch_shapes=[
            pltpu.VMEM((2 * half, n * lanes), BF),
            pltpu.VMEM((n_tok, n * lanes), BF),
            pltpu.SemaphoreType.DMA((n, 3)),
            pltpu.SemaphoreType.DMA((4, 3)),
        ],
        compiler_params=pltpu.CompilerParams(vmem_limit_bytes=24 << 20),
        cost_estimate=pl.CostEstimate(
            flops=2 * 2 * half * n * lanes * n_tok, bytes_accessed=4 << 20, transcendentals=0
        ),
        name="down_far" if far else "down_near",
    )(where, scale, *hidden, *pieces, *([] if far else [routed]))


def exchanged(
    tokens,
    expert_ids,
    route_gates,
    shared_gate_vec,
    w_shared_gate,
    w_shared_up,
    w_shared_down_t,
    w_expert_gate_t,
    w_expert_up_t,
    w_expert_down,
):
    z, t, g = lax.axis_index("dp"), lax.axis_index("tensor"), lax.axis_index("groups")
    n_dp, n_t, n_g = lax.axis_size("dp"), lax.axis_size("tensor"), lax.axis_size("groups")
    where = jnp.stack([z, t, g]).astype(jnp.int32)
    rows, d = tokens.shape
    top = expert_ids.shape[1]
    width = w_shared_gate.shape[1] // (n_dp * n_g)

    some = where[0] >= 0

    def apart(step, *operands):
        shapes = jax.eval_shape(step, *operands)
        empty = lambda *_: jax.tree.map(lambda a: jnp.zeros(a.shape, a.dtype), shapes)
        return lax.cond(some, step, empty, *operands)

    def first_step(mine, *weights):
        packed = pack(where, *weights, width)
        over_z = jnp.stack([mine] + [swap(mine, "dp", k) for k in range(1, n_dp)])
        return over_z, packed

    over_z, packed = apart(
        first_step,
        token_rows(where, tokens, expert_ids.T, route_gates.T),
        w_shared_gate,
        w_shared_up,
        w_shared_down_t,
    )
    gu = [packed[0]] + [swap(packed[k], "dp", k) for k in range(1, n_dp)]

    def cross(piece, r):
        route = [(i * n_t + j, (j ^ r) * n_t + i) for i in range(n_dp) for j in range(n_t)]
        return lax.ppermute(piece, ("dp", "tensor"), route)

    def routed_step(q, *weights):
        over_x, other = swap(q, "tensor", 2), swap(q, "groups", 1)
        over_core = swap(q, "tensor", 1)
        over_x, other = lax.optimization_barrier((over_x, other))
        over_both, other = lax.optimization_barrier((swap(over_x, "tensor", 1), other))
        other_x = swap(other, "tensor", 2)
        own = (q, over_core, over_x, over_both)
        give, keep = routed_experts(where, own, *weights, top)
        other, other_x, give = lax.optimization_barrier((other, other_x, give))
        others = (other, swap(other, "tensor", 1), other_x, swap(other_x, "tensor", 1))
        return own, others, give, keep

    tok_own, tok_other, give, keep = apart(
        routed_step, over_z, w_expert_gate_t, w_expert_up_t, w_expert_down
    )
    vec = shared_gate_vec[None, :]
    far_hidden, far_scale = shared_hidden(where, tok_other, gu, vec, give, width)

    def gather_step(h, tokens_here, pieces, out, kept):
        over_x, over_core = swap(h, "tensor", 2), swap(h, "tensor", 1)
        near = shared_hidden(where, tokens_here, pieces, vec, h, width)
        over_x, over_core, out, near = lax.optimization_barrier((over_x, over_core, out, near))
        got = swap(out, "tensor", 1).astype(F32)
        sums = kept[0] + got[0], (kept[1] + got[1]).astype(BF)
        return [h, over_core, over_x, swap(over_x, "tensor", 1)], near, sums

    far_hidden, first = lax.optimization_barrier((far_hidden, cross(packed[n_dp], 0)))
    gathered, (near_hidden, near_scale), (routed, routed_far) = apart(
        gather_step, far_hidden, tok_own, gu, give, keep
    )
    near_x, near_core = swap(near_hidden, "tensor", 2), swap(near_hidden, "tensor", 1)
    down = [first] + [cross(packed[n_dp + r], r) for r in range(1, n_dp)]
    far = shared_down(where, down, gathered, far_scale, width, True, None)
    gathered = [near_hidden, near_core, near_x, swap(near_x, "tensor", 1)]
    near = shared_down(where, down, gathered, near_scale, width, False, routed)
    total = near + swap(far, "groups", 1).astype(F32) + swap(routed_far, "tensor", 2).astype(F32)
    done = total[:, :rows]
    for k in range(1, n_dp):
        piece = total[:, rows * k : rows * (k + 1)].astype(BF)
        done = done + swap(piece, "dp", k).astype(F32)
    return done.T.astype(BF)


def solution(mesh):
    sizes = mesh.shape

    def on_device(*args):
        d_part, ff = args[4].shape
        width = ff // (sizes["dp"] * sizes["groups"])
        fits = (
            sizes["dp"] == 4
            and sizes["tensor"] == 4
            and sizes["groups"] == 2
            and width % 128 == 64
            and d_part % 32 == 0
            and args[7].shape[2] % 256 == 0
            and args[1].shape[1] == 8
            and args[0].shape[0] % 128 == 0
        )
        return (exchanged if fits else general)(*args)

    return jax.shard_map(
        on_device,
        mesh=mesh,
        in_specs=(
            P(("groups", "dp"), None),
            P(("groups", "dp"), None),
            P(("groups", "dp"), None),
            P(),
            P("dp", "tensor"),
            P("dp", "tensor"),
            P("dp", "tensor"),
            P("dp", "tensor", None),
            P("dp", "tensor", None),
            P("dp", "tensor", None),
        ),
        out_specs=P(("groups", "dp"), "tensor"),
        check_vma=False,
    )
```

```python
import jax
import jax.numpy as jnp
from jax import lax
from jax.experimental import pallas as pl
from jax.experimental.pallas import tpu as pltpu
from jax.sharding import PartitionSpec as P

CAP = 48
BF = jnp.bfloat16
F32 = jnp.float32


def slot_places(expert_ids, experts):
    flat_ids = expert_ids.reshape(-1)
    labels = jnp.arange(experts, dtype=jnp.int32)
    onehot = (flat_ids[:, None] == labels[None, :]).astype(jnp.int32)
    before = jnp.cumsum(onehot, axis=0, dtype=jnp.int32) - onehot
    return (jnp.sum(before * onehot, axis=1, dtype=jnp.int32), flat_ids)


def general(
    tokens,
    expert_ids,
    route_gates,
    shared_gate_vec,
    w_shared_gate,
    w_shared_up,
    w_shared_down_t,
    w_expert_gate_t,
    w_expert_up_t,
    w_expert_down,
):
    n_dp = lax.axis_size("dp")
    row_count, model_width = tokens.shape
    top_k = expert_ids.shape[1]
    exp_dev = w_expert_gate_t.shape[0]
    experts = exp_dev * n_dp
    portion_gate = lax.all_gather(w_shared_gate, "dp", axis=0, tiled=True)
    portion_up = lax.all_gather(w_shared_up, "dp", axis=0, tiled=True)
    portion_down = lax.all_gather(w_shared_down_t, "dp", axis=0, tiled=True)
    acc_gate = jnp.dot(tokens, portion_gate, preferred_element_type=jnp.float32)
    acc_up = jnp.dot(tokens, portion_up, preferred_element_type=jnp.float32)
    shared_hidden = (jax.nn.silu(acc_gate) * acc_up).astype(jnp.bfloat16)
    shared_part = lax.dot_general(
        shared_hidden, portion_down, (((1,), (1,)), ((), ())), preferred_element_type=jnp.float32
    )
    shared_scale = jax.nn.sigmoid(
        jnp.dot(tokens, shared_gate_vec, preferred_element_type=jnp.float32)
    )
    places, flat_ids = slot_places(expert_ids, experts)
    target = flat_ids * CAP + places
    source_rows = jnp.arange(row_count * top_k, dtype=jnp.int32) // top_k
    outgoing = (
        jnp.zeros((experts * CAP, model_width), jnp.bfloat16).at[target].set(tokens[source_rows])
    )
    arrived = lax.all_to_all(
        outgoing.reshape(n_dp, exp_dev * CAP, model_width),
        "dp",
        split_axis=0,
        concat_axis=0,
        tiled=True,
    )
    arrived = arrived.reshape(n_dp, exp_dev, CAP, model_width)
    ex_gate = jnp.einsum(
        "sjcd,jfd->sjcf", arrived, w_expert_gate_t, preferred_element_type=jnp.float32
    )
    ex_up = jnp.einsum("sjcd,jfd->sjcf", arrived, w_expert_up_t, preferred_element_type=jnp.float32)
    ex_hidden = (jax.nn.silu(ex_gate) * ex_up).astype(jnp.bfloat16)
    ex_part = jnp.einsum(
        "sjcf,jfd->sjcd", ex_hidden, w_expert_down, preferred_element_type=jnp.float32
    )
    returned = lax.all_to_all(
        ex_part.reshape(n_dp, exp_dev * CAP, model_width),
        "dp",
        split_axis=0,
        concat_axis=0,
        tiled=True,
    )
    returned = returned.reshape(experts * CAP, model_width)
    picked = returned[target].reshape(row_count, top_k, model_width)
    routed = jnp.sum(picked * route_gates[:, :, None], axis=1)
    combined = shared_scale[:, None] * shared_part + routed
    return lax.psum_scatter(combined, "tensor", scatter_dimension=1, tiled=True).astype(
        jnp.bfloat16
    )


def swap(x, axis, bit):
    n = lax.axis_size(axis)
    return lax.ppermute(x, axis, [(i, i ^ bit) for i in range(n)])


def vmem_full(a):
    return pl.BlockSpec(a.shape, lambda *_: (0,) * a.ndim)


ANY = pl.BlockSpec(memory_space=pl.ANY)
FULL = 60 << 20
SMEM = pl.BlockSpec(memory_space=pltpu.SMEM)


def run_all(copies):
    for c in copies:
        c.start()
    for c in copies:
        c.wait()


def token_rows(where, tokens, ids_t, gates_t):
    rows, d = tokens.shape
    top = ids_t.shape[0]
    quarter = rows // 4

    def kernel(where_ref, tok_ref, ids_ref, gates_ref, mine, tags, sem):
        at = pl.multiple_of(where_ref[1] * quarter, quarter)
        copy = pltpu.make_async_copy(
            tok_ref.at[pl.ds(at, quarter)], mine.at[:, pl.ds(0, d)], sem
        )
        copy.start()
        gates = gates_ref[...]
        high = gates.astype(BF).astype(F32)
        lines = [ids_ref[...].astype(F32), high, gates - high]
        lines.append(jnp.zeros((128 - 3 * top, rows), F32))
        tags[...] = jnp.concatenate(lines, axis=0).T
        mine[:, pl.ds(d, 128)] = tags[pl.ds(at, quarter), :].astype(BF)
        copy.wait()

    vm = pl.BlockSpec(memory_space=pltpu.VMEM)
    return pl.pallas_call(
        kernel,
        out_shape=jax.ShapeDtypeStruct((quarter, d + 128), BF),
        in_specs=[SMEM, ANY, vm, vm],
        out_specs=vm,
        scratch_shapes=[pltpu.VMEM((rows, 128), F32), pltpu.SemaphoreType.DMA],
        compiler_params=pltpu.CompilerParams(vmem_limit_bytes=FULL),
        name="token_rows",
    )(where, tokens, ids_t, gates_t)


def pack(where, wg, wu, wd, width):
    d_part, ff = wg.shape
    n = ff // (2 * width)
    whole = width - 64
    half = d_part // 2

    def kernel(where_ref, g_ref, u_ref, d_ref, *rest):
        outs_gu, outs_d = rest[:n], rest[n : 2 * n]
        gu_buf, d_buf, gu_mid, d_mid, in_sem, out_sem = rest[2 * n :]
        z, t, g = where_ref[0], where_ref[1], where_ref[2]
        side = g * (width + 64)
        loads = []
        for k in range(n):
            start = (z ^ k) * (2 * width)
            wide = pl.multiple_of(start + side, 128)
            mid = pl.multiple_of(start + whole, 128)
            jobs = []
            for m, ref in enumerate((g_ref, u_ref)):
                lane = 0 if m == 0 else width + 64
                jobs.append((ref.at[:, pl.ds(wide, whole)], gu_buf.at[k, :, pl.ds(lane, whole)]))
                jobs.append((ref.at[:, pl.ds(mid, 128)], gu_mid.at[k, m]))
            loads.append(jobs)
        for r in range(n):
            start = (t ^ r) * (2 * width)
            wide = pl.multiple_of(start + side, 128)
            mid = pl.multiple_of(start + whole, 128)
            jobs = []
            for m in range(2):
                lane = 0 if m == 0 else width + 64
                part = d_ref.at[pl.ds(m * half, half)]
                jobs.append((part.at[:, pl.ds(wide, whole)], d_buf.at[r, :, pl.ds(lane, whole)]))
                jobs.append((part.at[:, pl.ds(mid, 128)], d_mid.at[r, m]))
            loads.append(jobs)
        order = [1, 2, 3, 0, n, n + 1, n + 2, n + 3]
        copies = {}
        for i in order:
            copies[i] = [
                pltpu.make_async_copy(s, d, in_sem.at[i, j]) for j, (s, d) in enumerate(loads[i])
            ]
            for c in copies[i]:
                c.start()
        stores = []
        for i in order:
            for c in copies[i]:
                c.wait()
            buf, mids, out = (gu_buf, gu_mid, outs_gu[i]) if i < n else (d_buf, d_mid, outs_d[i - n])
            p = i % n
            first = pltpu.roll(mids[p, 0].astype(F32), 64 * g, 1)
            second = pltpu.roll(mids[p, 1].astype(F32), 64 * (1 - g), 1)
            lane = lax.broadcasted_iota(jnp.int32, first.shape, 1)
            buf[p, :, pl.ds(whole, 128)] = jnp.where(lane < 64, first, second).astype(BF)
            stores.append(pltpu.make_async_copy(buf.at[p], out, out_sem.at[i]))
            stores[-1].start()
        for c in stores:
            c.wait()

    return pl.pallas_call(
        kernel,
        out_shape=[jax.ShapeDtypeStruct((d_part, 2 * width), BF)] * n
        + [jax.ShapeDtypeStruct((half, 2 * width), BF)] * n,
        in_specs=[SMEM, ANY, ANY, ANY],
        out_specs=[ANY] * (2 * n),
        scratch_shapes=[
            pltpu.VMEM((n, d_part, 2 * width), BF),
            pltpu.VMEM((n, half, 2 * width), BF),
            pltpu.VMEM((n, 2, d_part, 128), BF),
            pltpu.VMEM((n, 2, half, 128), BF),
            pltpu.SemaphoreType.DMA((2 * n, 4)),
            pltpu.SemaphoreType.DMA((2 * n,)),
        ],
        compiler_params=pltpu.CompilerParams(vmem_limit_bytes=FULL),
        cost_estimate=pl.CostEstimate(flops=0, bytes_accessed=8 << 20, transcendentals=0),
        name="pack",
    )(where, wg, wu, wd)


def token_copies(where_ref, refs, rows_ref, info_ref, sem, base):
    t = where_ref[1]
    n_dp, quarter, _ = refs[0].shape
    d = rows_ref.shape[1]
    copies = []
    for k in range(n_dp):
        jobs = []
        for b, ref in enumerate(refs):
            row = pl.multiple_of(base + k * 4 * quarter + (t ^ b) * quarter, quarter)
            src = ref.at[k]
            jobs.append((src.at[:, pl.ds(0, d)], rows_ref.at[pl.ds(row, quarter)]))
            if info_ref is not None:
                jobs.append((src.at[:, pl.ds(d, 128)], info_ref.at[pl.ds(row, quarter)]))
        copies.append(
            [pltpu.make_async_copy(x, y, sem.at[k, j]) for j, (x, y) in enumerate(jobs)]
        )
    return copies


def routed_experts(where, spread_tokens, eg, eu, ed, top):
    e_dev, ff_e, d = eg.shape
    n_dp, quarter, _ = spread_tokens[0].shape
    block = 4 * quarter
    n_tok = n_dp * block
    part = d // 4
    pairs = n_dp // 2
    seg = 2 * CAP
    side = e_dev * seg

    def kernel(where_ref, *rest):
        refs = rest[:4]
        g_ref, u_ref, w_ref, give, keep, tok, info, back, moved, gate_of, acc_t, sem = rest[4:]
        e = pl.program_id(0)
        z, t = where_ref[0], where_ref[1]

        @pl.when(e == 0)
        def _():
            run_all(sum(token_copies(where_ref, refs, tok, info, sem, 0), []))
            tags = info[...].astype(F32)
            lane = lax.broadcasted_iota(jnp.int32, tags.shape, 1)
            weight = pltpu.roll(tags, 128 - top, 1) + pltpu.roll(tags, 128 - 2 * top, 1)
            chosen = jnp.zeros(tags.shape, F32)
            gates = jnp.zeros(tags.shape, F32)
            for i in range(e_dev):
                hit = (tags == (z * e_dev + i).astype(F32)) & (lane < top)
                has = jnp.sum(jnp.where(hit, 1.0, 0.0), axis=1, keepdims=True)
                gate = jnp.sum(jnp.where(hit, weight, 0.0), axis=1, keepdims=True)
                chosen = jnp.where(lane == i, has, chosen)
                gates = jnp.where(lane == i, gate, gates)
            row = lax.broadcasted_iota(jnp.int32, (block, block), 0)
            col = lax.broadcasted_iota(jnp.int32, (block, block), 1)
            earlier = jnp.where(col < row, 1.0, 0.0).astype(BF)
            for p in range(pairs):
                slots = []
                for b in range(2):
                    lo = (2 * p + b) * block
                    mine = chosen[lo : lo + block]
                    before = jnp.dot(earlier, mine.astype(BF), preferred_element_type=F32)
                    slots.append(jnp.where(mine > 0.5, before + b * CAP, -1.0))
                slot_t = jnp.concatenate(slots, axis=0).T
                gate_t = gates[2 * p * block : 2 * (p + 1) * block].T
                picks = []
                for i in range(e_dev):
                    spot = lax.broadcasted_iota(jnp.int32, (seg, 2 * block), 0).astype(F32)
                    hit = spot == slot_t[i : i + 1, :]
                    g = jnp.sum(jnp.where(hit, gate_t[i : i + 1, :], 0.0), axis=1, keepdims=True)
                    gate_of[pl.ds(p * side + i * seg, seg), :] = jnp.broadcast_to(g, (seg, 128))
                    picks.append(jnp.where(hit, 1.0, 0.0))
                pick = jnp.concatenate(picks, axis=0)
                back[p] = pick.T.astype(BF)
                moved[pl.ds(p * side, side), :] = jnp.dot(
                    pick.astype(BF),
                    tok[pl.ds(2 * p * block, 2 * block), :],
                    preferred_element_type=F32,
                ).astype(BF)

        spots = [pl.ds(pl.multiple_of(p * side + e * seg, seg), seg) for p in range(pairs)]
        x = jnp.concatenate([moved[s, :] for s in spots], axis=0)
        dims = (((1,), (1,)), ((), ()))
        gate = lax.dot_general(x, g_ref[0], dims, preferred_element_type=F32)
        up = lax.dot_general(x, u_ref[0], dims, preferred_element_type=F32)
        hidden = (gate * jax.nn.sigmoid(gate) * up).astype(BF)
        out = jnp.dot(hidden, w_ref[0], preferred_element_type=F32)
        for p, s in enumerate(spots):
            moved[s, :] = (gate_of[s, :1] * out[p * seg : (p + 1) * seg]).astype(BF)

        @pl.when(e == e_dev - 1)
        def _():
            for p in range(pairs):
                for i in range(d // 256):
                    sums = jnp.dot(
                        back[p],
                        moved[pl.ds(p * side, side), pl.ds(256 * i, 256)],
                        preferred_element_type=F32,
                    )
                    acc_t[pl.ds(256 * i, 256), pl.ds(2 * p * block, 2 * block)] = sums.T
            for b in range(2):
                mine = pl.multiple_of((t ^ (2 * b)) * part, part)
                theirs = pl.multiple_of((t ^ (2 * b + 1)) * part, part)
                keep[b] = acc_t[pl.ds(mine, part), :]
                give[b] = acc_t[pl.ds(theirs, part), :].astype(BF)

    weights = pl.BlockSpec((1, ff_e, d), lambda e: (e, 0, 0))
    return pl.pallas_call(
        kernel,
        grid=(e_dev,),
        out_shape=[
            jax.ShapeDtypeStruct((2, part, n_tok), BF),
            jax.ShapeDtypeStruct((2, part, n_tok), F32),
        ],
        in_specs=[SMEM] + [ANY] * 4 + [weights, weights, weights],
        out_specs=[
            pl.BlockSpec((2, part, n_tok), lambda e: (0, 0, 0)),
            pl.BlockSpec((2, part, n_tok), lambda e: (0, 0, 0)),
        ],
        scratch_shapes=[
            pltpu.VMEM((n_tok, d), BF),
            pltpu.VMEM((n_tok, 128), BF),
            pltpu.VMEM((pairs, 2 * block, side), BF),
            pltpu.VMEM((pairs * side, d), BF),
            pltpu.VMEM((pairs * side, 128), F32),
            pltpu.VMEM((d, n_tok), F32),
            pltpu.SemaphoreType.DMA((n_dp, 8)),
        ],
        compiler_params=pltpu.CompilerParams(vmem_limit_bytes=52 << 20),
        cost_estimate=pl.CostEstimate(
            flops=6 * pairs * side * ff_e * d,
            bytes_accessed=6 * e_dev * ff_e * d,
            transcendentals=pairs * side * ff_e,
        ),
        name="routed",
    )(where, *spread_tokens, eg, eu, ed)


def shared_hidden(where, tokens, pieces, vec, after, width):
    d_part = pieces[0].shape[0]
    n = len(pieces)
    d = n * d_part
    n_dp, quarter, _ = tokens[0].shape
    n_tok = n_dp * quarter * 4
    half = n_tok // 2
    whole = width - 64

    def kernel(where_ref, *rest):
        refs, vec_ref, p_refs = rest[:4], rest[4], rest[5 : 5 + n]
        hid, scale, tok, w, tok_sem, w_sem = rest[6 + n :]
        z = where_ref[0]
        w_copies = []
        for k in range(n):
            row = pl.multiple_of((z ^ k) * d_part, d_part)
            w_copies.append(
                pltpu.make_async_copy(p_refs[k], w.at[pl.ds(row, d_part)], w_sem.at[k])
            )
        copies = token_copies(where_ref, refs, tok, None, tok_sem, 0)
        for batch in [w_copies] + copies:
            for c in batch:
                c.start()
        dims = (((1,), (1,)), ((), ()))
        lines = jnp.broadcast_to(vec_ref[...], (8, d))
        for c in w_copies:
            c.wait()
        mids = []
        for side in range(2):
            for k in range(side * n_dp // 2, (side + 1) * n_dp // 2):
                for c in copies[k]:
                    c.wait()
            rows = pl.ds(side * half, half)
            x = tok[rows, :]
            acc = jnp.dot(x, w[...], preferred_element_type=F32)
            gate_mid = acc[:, whole : whole + 128]
            up_mid = pltpu.roll(gate_mid, 64, 1)
            gate, up = acc[:, :whole], acc[:, width + 64 :]
            line = lax.dot_general(lines, x, dims, preferred_element_type=F32)
            scale[:, rows] = jax.nn.sigmoid(line[:1])
            at = pl.ds(side * (width + 64), whole)
            hid[:, at] = (gate * jax.nn.sigmoid(gate) * up).astype(BF)
            mids.append(gate_mid * jax.nn.sigmoid(gate_mid) * up_mid)
        lane = lax.broadcasted_iota(jnp.int32, mids[0].shape, 1)
        mid = jnp.where(lane < 64, mids[0], pltpu.roll(mids[1], 64, 1))
        hid[:, pl.ds(whole, 128)] = mid.astype(BF)

    vm = pl.BlockSpec(memory_space=pltpu.VMEM)
    return pl.pallas_call(
        kernel,
        out_shape=[
            jax.ShapeDtypeStruct((half, 2 * width), BF),
            jax.ShapeDtypeStruct((1, n_tok), F32),
        ],
        in_specs=[SMEM] + [ANY] * 4 + [vm] + [ANY] * (n + 1),
        out_specs=[vm] * 2,
        scratch_shapes=[
            pltpu.VMEM((n_tok, d), BF),
            pltpu.VMEM((d, 2 * width), BF),
            pltpu.SemaphoreType.DMA((n_dp, 4)),
            pltpu.SemaphoreType.DMA((n,)),
        ],
        compiler_params=pltpu.CompilerParams(vmem_limit_bytes=24 << 20),
        cost_estimate=pl.CostEstimate(
            flops=2 * n_tok * d * 2 * width,
            bytes_accessed=4 << 20,
            transcendentals=n_tok * width,
        ),
        name="shared_hidden",
    )(where, *tokens, vec, *pieces, after)


def shared_down(where, pieces, hidden, scale, width, far, routed):
    n = len(pieces)
    half = pieces[0].shape[0]
    whole = width - 64
    lanes = whole + 128
    rows_h = hidden[0].shape[0]
    n_tok = 2 * rows_h

    def kernel(where_ref, scale_ref, *rest):
        h_refs, p_refs = rest[:4], rest[4 : 4 + n]
        if far:
            out_ref, w, h, w_sem, h_sem = rest[4 + n :]
        else:
            routed_ref, out_ref, w, h, w_sem, h_sem = rest[4 + n :]
        z, t = where_ref[0], where_ref[1]
        copies = []
        for r in range(n):
            jobs = (
                (p_refs[r].at[:, pl.ds(0, lanes)], w.at[pl.ds(0, half), pl.ds(lanes * r, lanes)]),
                (
                    p_refs[r].at[:, pl.ds(lanes, whole)],
                    w.at[pl.ds(half, half), pl.ds(lanes * r, whole)],
                ),
                (
                    p_refs[r].at[:, pl.ds(whole, 128)],
                    w.at[pl.ds(half, half), pl.ds(lanes * r + whole, 128)],
                ),
            )
            for j, (s, d) in enumerate(jobs):
                copies.append(pltpu.make_async_copy(s, d, w_sem.at[r, j]))
        for m in range(4):
            at = pl.multiple_of((z ^ t ^ m) * lanes, lanes)
            top, bottom = h.at[pl.ds(0, rows_h)], h.at[pl.ds(rows_h, rows_h)]
            jobs = (
                (h_refs[m].at[:, pl.ds(0, lanes)], top.at[:, pl.ds(at, lanes)]),
                (h_refs[m].at[:, pl.ds(lanes, whole)], bottom.at[:, pl.ds(at, whole)]),
                (h_refs[m].at[:, pl.ds(whole, 128)], bottom.at[:, pl.ds(at + whole, 128)]),
            )
            for j, (s, d) in enumerate(jobs):
                copies.append(pltpu.make_async_copy(s, d, h_sem.at[m, j]))
        run_all(copies)
        low = lax.broadcasted_iota(jnp.int32, (half, 128), 1) < 64
        low_h = lax.broadcasted_iota(jnp.int32, (rows_h, 128), 1) < 64
        for r in range(n):
            at = pl.ds(lanes * r + whole, 128)
            for i in range(2):
                rows = pl.ds(half * i, half)
                mask = low if i == 0 else ~low
                w[rows, at] = jnp.where(mask, w[rows, at].astype(F32), 0.0).astype(BF)
            for i in range(2):
                rows = pl.ds(rows_h * i, rows_h)
                mid = h[rows, at].astype(F32)
                mask = low_h if i == 0 else ~low_h
                h[rows, at] = jnp.where(mask, mid, pltpu.roll(mid, 64, 1)).astype(BF)
        dims = (((1,), (1,)), ((), ()))
        out = lax.dot_general(w[...], h[...], dims, preferred_element_type=F32)
        if far:
            out_ref[...] = (out * scale_ref[...]).astype(BF)
        else:
            out_ref[...] = out * scale_ref[...] + routed_ref[...]

    vm = pl.BlockSpec(memory_space=pltpu.VMEM)
    return pl.pallas_call(
        kernel,
        out_shape=jax.ShapeDtypeStruct((2 * half, n_tok), BF if far else F32),
        in_specs=[SMEM, vm] + [ANY] * (4 + n) + ([] if far else [vm]),
        out_specs=vm,
        scratch_shapes=[
            pltpu.VMEM((2 * half, n * lanes), BF),
            pltpu.VMEM((n_tok, n * lanes), BF),
            pltpu.SemaphoreType.DMA((n, 3)),
            pltpu.SemaphoreType.DMA((4, 3)),
        ],
        compiler_params=pltpu.CompilerParams(vmem_limit_bytes=24 << 20),
        cost_estimate=pl.CostEstimate(
            flops=2 * 2 * half * n * lanes * n_tok, bytes_accessed=4 << 20, transcendentals=0
        ),
        name="down_far" if far else "down_near",
    )(where, scale, *hidden, *pieces, *([] if far else [routed]))


def exchanged(
    tokens,
    expert_ids,
    route_gates,
    shared_gate_vec,
    w_shared_gate,
    w_shared_up,
    w_shared_down_t,
    w_expert_gate_t,
    w_expert_up_t,
    w_expert_down,
):
    z, t, g = lax.axis_index("dp"), lax.axis_index("tensor"), lax.axis_index("groups")
    n_dp, n_t, n_g = lax.axis_size("dp"), lax.axis_size("tensor"), lax.axis_size("groups")
    where = jnp.stack([z, t, g]).astype(jnp.int32)
    rows, d = tokens.shape
    top = expert_ids.shape[1]
    width = w_shared_gate.shape[1] // (n_dp * n_g)

    some = where[0] >= 0

    def apart(step, *operands):
        shapes = jax.eval_shape(step, *operands)
        empty = lambda *_: jax.tree.map(lambda a: jnp.zeros(a.shape, a.dtype), shapes)
        return lax.cond(some, step, empty, *operands)

    def first_step(mine, *weights):
        packed = pack(where, *weights, width)
        over_z = jnp.stack([mine] + [swap(mine, "dp", k) for k in range(1, n_dp)])
        return over_z, packed

    over_z, packed = apart(
        first_step,
        token_rows(where, tokens, expert_ids.T, route_gates.T),
        w_shared_gate,
        w_shared_up,
        w_shared_down_t,
    )
    gu = [packed[0]] + [swap(packed[k], "dp", k) for k in range(1, n_dp)]

    def cross(piece, r):
        route = [(i * n_t + j, (j ^ r) * n_t + i) for i in range(n_dp) for j in range(n_t)]
        return lax.ppermute(piece, ("dp", "tensor"), route)

    def routed_step(q, *weights):
        over_x, other = swap(q, "tensor", 2), swap(q, "groups", 1)
        over_core = swap(q, "tensor", 1)
        over_x, other = lax.optimization_barrier((over_x, other))
        over_both, other = lax.optimization_barrier((swap(over_x, "tensor", 1), other))
        other_x = swap(other, "tensor", 2)
        own = (q, over_core, over_x, over_both)
        give, keep = routed_experts(where, own, *weights, top)
        other, other_x, give = lax.optimization_barrier((other, other_x, give))
        others = (other, swap(other, "tensor", 1), other_x, swap(other_x, "tensor", 1))
        return own, others, give, keep

    tok_own, tok_other, give, keep = apart(
        routed_step, over_z, w_expert_gate_t, w_expert_up_t, w_expert_down
    )
    vec = shared_gate_vec[None, :]
    far_hidden, far_scale = shared_hidden(where, tok_other, gu, vec, give, width)

    def gather_step(h, tokens_here, pieces, out, kept):
        over_x, over_core = swap(h, "tensor", 2), swap(h, "tensor", 1)
        near = shared_hidden(where, tokens_here, pieces, vec, h, width)
        over_x, over_core, out, near = lax.optimization_barrier((over_x, over_core, out, near))
        got = swap(out, "tensor", 1).astype(F32)
        sums = kept[0] + got[0], (kept[1] + got[1]).astype(BF)
        return [h, over_core, over_x, swap(over_x, "tensor", 1)], near, sums

    far_hidden, first = lax.optimization_barrier((far_hidden, cross(packed[2 * n_dp - 1], n_dp - 1)))
    gathered, (near_hidden, near_scale), (routed, routed_far) = apart(
        gather_step, far_hidden, tok_own, gu, give, keep
    )
    near_x, near_core = swap(near_hidden, "tensor", 2), swap(near_hidden, "tensor", 1)
    down = [cross(packed[n_dp + r], r) for r in range(n_dp - 1)] + [first]
    far = shared_down(where, down, gathered, far_scale, width, True, None)
    gathered = [near_hidden, near_core, near_x, swap(near_x, "tensor", 1)]
    near = shared_down(where, down, gathered, near_scale, width, False, routed)
    total = near + swap(far, "groups", 1).astype(F32) + swap(routed_far, "tensor", 2).astype(F32)
    done = total[:, :rows]
    for k in range(1, n_dp):
        piece = total[:, rows * k : rows * (k + 1)].astype(BF)
        done = done + swap(piece, "dp", k).astype(F32)
    return done.T.astype(BF)


def solution(mesh):
    sizes = mesh.shape

    def on_device(*args):
        d_part, ff = args[4].shape
        width = ff // (sizes["dp"] * sizes["groups"])
        fits = (
            sizes["dp"] == 4
            and sizes["tensor"] == 4
            and sizes["groups"] == 2
            and width % 128 == 64
            and d_part % 32 == 0
            and args[7].shape[2] % 256 == 0
            and args[1].shape[1] == 8
            and args[0].shape[0] % 128 == 0
        )
        return (exchanged if fits else general)(*args)

    return jax.shard_map(
        on_device,
        mesh=mesh,
        in_specs=(
            P(("groups", "dp"), None),
            P(("groups", "dp"), None),
            P(("groups", "dp"), None),
            P(),
            P("dp", "tensor"),
            P("dp", "tensor"),
            P("dp", "tensor"),
            P("dp", "tensor", None),
            P("dp", "tensor", None),
            P("dp", "tensor", None),
        ),
        out_specs=P(("groups", "dp"), "tensor"),
        check_vma=False,
    )
```
